32 devices in a mesh: dp: 8 (over z, core), proto: 4 (over y, x).
Axes of the slice: x: 2, y: 2, z: 4, core: 2. Of those that a mesh axis runs over, the one named last changes fastest.
Arguments:
- teacher_feat: bfloat16 [1024, 256], P('dp'), may hold values from -8 to 8
- student_feat: bfloat16 [5120, 256], P('dp'), may hold values from -8 to 8
- teacher_weight: bfloat16 [256, 131072], P(None, 'proto'), may hold values from -0.375 to 0.375
- head_weight: bfloat16 [256, 131072], P(None, 'proto'), may hold values from -0.375 to 0.375
- pairing: int32 [5120], P('dp'), may hold values from 0 to 1023, as said below
Outputs:
- student_grad: float32 [5120, 256], P('dp', 'proto')
- head_grad: float32 [256, 131072], P('dp', 'proto')
The draws below stay inside these ranges and needn't reach their ends.
Inputs may be any that keep to these rules, and one draw needn't show every extreme that they name: `pairing`: row r among the 640 student rows of one index j of dp is crop r // 64 of image m = r mod 64; it names teacher row j * 128 + m + 64 * v with view v of 0 or 1; crop 0 takes view 1 and crop 1 takes view 0.
All inputs are finite; a program needn't handle non-finite values.
Results may differ from the reference program's by a relative error of at most 0.0022.
Values sent between devices are 32-bit elements; how exact they have to be, the bound alone decides.
A program may use at most 320 MiB of HBM per device.

```python
import math
import jax
import jax.numpy as jnp
from jax import lax

DIM = 256
PROTOS = 131072
IMG_DEV = 64
ITERS = 3
TEACH_DEV = 128
STUD_DEV = 640
TEACHER = 1024
STUDENT = 5120


def shared_directions(key):
    return jax.random.truncated_normal(jax.random.fold_in(key, 31), -2.5, 2.5, (16, DIM), jnp.float32)


def prototype_columns(key, salt):
    directions = shared_directions(key)
    columns = jnp.arange(PROTOS, dtype=jnp.int32)
    group = (columns // (PROTOS // 16)).astype(jnp.int32)
    centers = jnp.take(directions, group, axis=0).T
    noise = jax.random.truncated_normal(jax.random.fold_in(key, salt), -2.5, 2.5, (DIM, PROTOS), jnp.float32)
    strength = jax.random.uniform(jax.random.fold_in(key, salt + 1), (1, PROTOS), jnp.float32, 0.4, 0.8)
    values = (noise + strength * centers) / math.sqrt(DIM)
    return jnp.clip(values, -0.375, 0.375).astype(jnp.bfloat16)


def draw_teacher_weight(key, part):
    return prototype_columns(key, 51)


def draw_head_weight(key, part):
    return prototype_columns(key, 61)


def draw_pairing(key, part):
    rows = jnp.arange(STUDENT, dtype=jnp.int32)
    block = rows // STUD_DEV
    within = rows % STUD_DEV
    image = within % IMG_DEV
    crop = within // IMG_DEV
    drawn = jax.random.randint(jax.random.fold_in(key, 11), (STUDENT,), 0, 2, dtype=jnp.int32)
    view = jnp.where(crop == 0, 1, jnp.where(crop == 1, 0, drawn))
    return (block * TEACH_DEV + image + IMG_DEV * view).astype(jnp.int32)


def draw_teacher_feat(key, part):
    directions = shared_directions(key)
    rows = jnp.arange(TEACHER, dtype=jnp.int32)
    which = (rows // TEACH_DEV * 7 % 16).astype(jnp.int32)
    centers = jnp.take(directions, which, axis=0)
    mixing = jax.random.uniform(jax.random.fold_in(key, 23), (TEACHER, 1), jnp.float32, 0.6, 1.2)
    noise = jax.random.truncated_normal(jax.random.fold_in(key, 24), -2.5, 2.5, (TEACHER, DIM), jnp.float32)
    values = (mixing * centers + noise) * 0.5
    return jnp.clip(values, -8.0, 8.0).astype(jnp.bfloat16)


def draw_student_feat(key, part):
    directions = shared_directions(key)
    which = jax.random.randint(jax.random.fold_in(key, 41), (STUDENT,), 0, 16, dtype=jnp.int32)
    centers = jnp.take(directions, which, axis=0)
    strength = jax.random.uniform(jax.random.fold_in(key, 42), (STUDENT, 1), jnp.float32, 0.5, 1.0)
    noise = jax.random.truncated_normal(jax.random.fold_in(key, 43), -2.5, 2.5, (STUDENT, DIM), jnp.float32)
    values = strength * centers + noise
    return jnp.clip(values, -8.0, 8.0).astype(jnp.bfloat16)


def setup_inputs(seed: int = 0) -> dict:
    splits = jax.random.split(jax.random.key(seed), 6)
    return {
        "teacher_feat": draw_teacher_feat(jax.random.fold_in(splits[5], 71), 0),
        "student_feat": draw_student_feat(jax.random.fold_in(splits[5], 71), 0),
        "teacher_weight": draw_teacher_weight(jax.random.fold_in(splits[5], 71), 0),
        "head_weight": draw_head_weight(jax.random.fold_in(splits[5], 71), 0),
        "pairing": draw_pairing(jax.random.fold_in(splits[5], 71), 0),
    }


tiny_eps = 1e-06
teacher_temp = 0.04
student_temp = 0.1

def unit_rows(values):
    floats = values.astype(jnp.float32)
    inverse = lax.rsqrt(lax.optimization_barrier(jnp.sum(floats * floats, axis=1, keepdims=True)) + tiny_eps)
    return (floats * inverse, inverse)

def unit_columns(values):
    floats = values.astype(jnp.float32)
    inverse = lax.rsqrt(lax.optimization_barrier(jnp.sum(floats * floats, axis=0, keepdims=True)) + tiny_eps)
    return (floats * inverse, inverse)

def reference(teacher_feat, student_feat, teacher_weight, head_weight, pairing):
    teach_rows = unit_rows(teacher_feat)[0].astype(jnp.bfloat16)
    teach_cols = unit_columns(teacher_weight)[0].astype(jnp.bfloat16)
    col_block = math.gcd(PROTOS, 8192)
    col_count = PROTOS // col_block
    teach_blocks = teach_cols.reshape(DIM, col_count, col_block).transpose(1, 0, 2)

    def block_expo(columns):
        return jnp.exp(jnp.dot(teach_rows, columns, preferred_element_type=jnp.float32) / teacher_temp)
    row_scale = jnp.ones((TEACHER,), jnp.float32)
    col_scale = jnp.ones((PROTOS,), jnp.float32)
    for iteration in range(ITERS):
        scales_now = row_scale

        def column_total(columns):
            return lax.optimization_barrier(jnp.sum(block_expo(columns) * scales_now[:, None], axis=0))
        col_total = lax.map(column_total, teach_blocks).reshape(PROTOS)
        col_scale = 1.0 / col_total
        scale_blocks = col_scale.reshape(col_count, col_block)

        def add_rows(carry, inputs):
            columns, scales = inputs
            return (carry + lax.optimization_barrier(jnp.sum(block_expo(columns) * scales[None, :], axis=1)), None)
        row_total, unused = lax.scan(add_rows, jnp.zeros((TEACHER,), jnp.float32), (teach_blocks, scale_blocks))
        row_scale = 1.0 / row_total
    stud_unit, stud_inverse = unit_rows(student_feat)
    stud_rows = stud_unit.astype(jnp.bfloat16)
    head_unit, head_inverse = unit_columns(head_weight)
    head_cols = head_unit.astype(jnp.bfloat16)
    row_block = math.gcd(STUDENT, 512)
    block_count = STUDENT // row_block

    def student_block(carry, inputs):
        unit_blk, inverse_blk, rows_blk, pair_blk = inputs
        logits = jnp.dot(rows_blk, head_cols, preferred_element_type=jnp.float32) / student_temp
        expo_s = jnp.exp(logits)
        totals = lax.optimization_barrier(jnp.sum(expo_s, axis=1))
        teach_pick = jnp.take(teach_rows, pair_blk, axis=0)
        picked = jnp.exp(jnp.dot(teach_pick, teach_cols, preferred_element_type=jnp.float32) / teacher_temp)
        picked = picked * jnp.take(row_scale, pair_blk)[:, None] * col_scale[None, :]
        grad_logits = ((expo_s / totals[:, None] - picked) / (student_temp * STUDENT)).astype(jnp.bfloat16)
        full = lax.dot_general(grad_logits, head_cols, (((1,), (1,)), ((), ())), preferred_element_type=jnp.float32)
        along = lax.optimization_barrier(jnp.sum(unit_blk * full, axis=1))
        feat_grad = (full - unit_blk * along[:, None]) * inverse_blk
        carry = carry + lax.dot_general(rows_blk, grad_logits, (((0,), (0,)), ((), ())), preferred_element_type=jnp.float32)
        return (carry, feat_grad)
    inputs = (stud_unit.reshape(block_count, row_block, DIM), stud_inverse.reshape(block_count, row_block, 1), stud_rows.reshape(block_count, row_block, DIM), pairing.astype(jnp.int32).reshape(block_count, row_block))
    head_sum, feats = lax.scan(student_block, jnp.zeros((DIM, PROTOS), jnp.float32), inputs)
    student_grad = feats.reshape(STUDENT, DIM)
    head_grad = (head_sum - head_unit * lax.optimization_barrier(jnp.sum(head_unit * head_sum, axis=0, keepdims=True))) * head_inverse
    return (student_grad, head_grad)
```

```python
import jax
import jax.numpy as jnp
from jax import lax
from jax.sharding import PartitionSpec as P

ITERS = 3


tiny_eps = 1e-06
teacher_temp = 0.04
student_temp = 0.1
BOTH = ("dp", "proto")


def unit_rows(values):
    floats = values.astype(jnp.float32)
    inverse = lax.rsqrt(jnp.sum(floats * floats, axis=1, keepdims=True) + tiny_eps)
    return (floats * inverse, inverse)


def unit_columns(values):
    floats = values.astype(jnp.float32)
    inverse = lax.rsqrt(jnp.sum(floats * floats, axis=0, keepdims=True) + tiny_eps)
    return (floats * inverse, inverse)


def dot(a, b, da, db):
    return lax.dot_general(a, b, (((da,), (db,)), ((), ())), preferred_element_type=jnp.float32)


def split_sum(values):
    high = values.astype(jnp.bfloat16)
    return high, (values - high.astype(jnp.float32)).astype(jnp.bfloat16)


def body(teacher_feat, student_feat, teacher_weight, head_weight, pairing):
    dp, me = lax.axis_size("dp"), lax.axis_index("dp")
    protos = lax.axis_size("proto")
    teach, width = teacher_feat.shape
    stud = student_feat.shape[0]
    images = teach // 2
    crops = stud // images
    mine = head_weight.shape[1] // dp
    scale = 1.0 / (student_temp * stud * dp)

    teach_unit = unit_rows(teacher_feat)[0]
    stud_unit, stud_inverse = unit_rows(student_feat)
    view = (pairing - me * teach) // images
    kept = stud_unit.astype(jnp.bfloat16).astype(jnp.float32).reshape(crops, images, width)
    second = (view == 1).reshape(crops, images, 1)
    pair_sums = jnp.concatenate(
        [jnp.sum(jnp.where(second, 0.0, kept), 0), jnp.sum(jnp.where(second, kept, 0.0), 0)], 0
    )
    packet = jnp.concatenate([stud_unit, teach_unit, pair_sums], 0)
    packet = lax.optimization_barrier(lax.all_gather(packet, "dp", axis=0, tiled=False))
    stud_rows = packet[:, :stud].reshape(dp * stud, width).astype(jnp.bfloat16)
    teach_rows = packet[:, stud : stud + teach].reshape(dp * teach, width).astype(jnp.bfloat16)
    sums = packet[:, stud + teach :].reshape(dp * teach, width)

    teach_cols = unit_columns(lax.dynamic_slice_in_dim(teacher_weight, me * mine, mine, 1))[0].astype(jnp.bfloat16)
    head_unit, head_inverse = unit_columns(lax.dynamic_slice_in_dim(head_weight, me * mine, mine, 1))
    head_cols = head_unit.astype(jnp.bfloat16)

    expo = jnp.exp(dot(teach_rows, teach_cols, 1, 0) / teacher_temp)
    expo_s = jnp.exp(dot(stud_rows, head_cols, 1, 0) / student_temp)
    totals = lax.psum(jnp.sum(expo_s, axis=1), BOTH)
    expo_s = expo_s.astype(jnp.bfloat16)
    raw = dot(expo_s, head_cols, 1, 1)

    row_scale = jnp.ones((expo.shape[0],), jnp.float32)
    for iteration in range(ITERS):
        col_scale = 1.0 / jnp.sum(expo * row_scale[:, None], axis=0)
        row_scale = 1.0 / lax.psum(jnp.sum(expo * col_scale[None, :], axis=1), BOTH)
    targets = (expo * row_scale[:, None] * col_scale[None, :]).astype(jnp.bfloat16)

    aim = dot(targets, head_cols, 1, 1)
    block = jnp.concatenate(
        [(raw / totals[:, None]).reshape(dp, stud, width), aim.reshape(dp, teach, width)], 1
    )
    block = lax.psum_scatter(block, "dp", scatter_dimension=0, tiled=False)
    block = lax.psum_scatter(block, "proto", scatter_dimension=1, tiled=True)
    share = width // protos
    offset = lax.axis_index("proto") * share
    aims = block[stud:].reshape(2, 1, images, share)
    picked = jnp.where(second, aims[1], aims[0]).reshape(stud, share)
    own_part = (block[:stud] - picked) * scale
    own_unit = lax.dynamic_slice_in_dim(stud_unit, offset, share, 1)
    along = lax.psum(jnp.sum(own_unit * own_part, axis=1), "proto")
    student_grad = (own_part - own_unit * along[:, None]) * stud_inverse

    scaled = (stud_rows.astype(jnp.float32) / totals[:, None]).astype(jnp.bfloat16)
    high, low = split_sum(sums)
    weight_grad = (dot(scaled, expo_s, 0, 0) - dot(high, targets, 0, 0) - dot(low, targets, 0, 0)) * scale
    inner = jnp.sum(head_unit * weight_grad, axis=0, keepdims=True)
    head_grad = (weight_grad - head_unit * inner) * head_inverse
    head_grad = lax.all_to_all(head_grad, "dp", split_axis=0, concat_axis=1, tiled=True)
    return (student_grad, head_grad)


def solution(mesh):
    return jax.shard_map(
        body,
        mesh=mesh,
        in_specs=(P("dp", None), P("dp", None), P(None, "proto"), P(None, "proto"), P("dp")),
        out_specs=(P("dp", "proto"), P("dp", "proto")),
        check_vma=False,
    )
```

```python
import functools
import math

import jax
import jax.numpy as jnp
from jax import lax
from jax.experimental import pallas as pl
from jax.experimental.pallas import tpu as pltpu
from jax.sharding import PartitionSpec as P

ITERS = 3


tiny_eps = 1e-06
teacher_temp = 0.04
student_temp = 0.1
BOTH = ("dp", "proto")


def unit_rows(values):
    floats = values.astype(jnp.float32)
    inverse = lax.rsqrt(jnp.sum(floats * floats, axis=1, keepdims=True) + tiny_eps)
    return (floats * inverse, inverse)


def unit_columns(values):
    floats = values.astype(jnp.float32)
    inverse = lax.rsqrt(jnp.sum(floats * floats, axis=0, keepdims=True) + tiny_eps)
    return (floats * inverse, inverse)


def dot(a, b, da, db):
    return lax.dot_general(a, b, (((da,), (db,)), ((), ())), preferred_element_type=jnp.float32)


def split_sum(values):
    high = values.astype(jnp.bfloat16)
    return high, (values - high.astype(jnp.float32)).astype(jnp.bfloat16)


LOG2E = math.log2(math.e)
MIB = 1 << 20


def diagonal():
    shape = (128, 128)
    return lax.broadcasted_iota(jnp.int32, shape, 0) == lax.broadcasted_iota(jnp.int32, shape, 1)


def to_lanes(column):
    return jnp.sum(jnp.where(diagonal(), column, 0.0), axis=0, keepdims=True)


def to_column(lanes):
    return jnp.sum(jnp.where(diagonal(), lanes, 0.0), axis=1, keepdims=True)


def chunks(size):
    step = min(size, 1024)
    return [(c, step) for c in range(0, size, step)]


def student_kernel(rows_ref, cols_ref, cols_t_ref, expo_ref, raw_ref, total_ref, kept_ref):
    rows = rows_ref[0].astype(jnp.bfloat16)
    kept_ref[...] = rows
    raw, total = None, None
    for start, step in chunks(cols_ref.shape[1]):
        logits = dot(rows, cols_ref[:, start : start + step], 1, 0)
        expo = jnp.exp2(logits * (LOG2E / student_temp))
        part = jnp.sum(expo, axis=1, keepdims=True)
        kept = expo.astype(jnp.bfloat16)
        expo_ref[:, start : start + step] = kept
        grad = dot(kept, cols_t_ref[start : start + step, :], 1, 0)
        total = part if total is None else total + part
        raw = grad if raw is None else raw + grad
    raw_ref[...] = raw
    for j in range(rows.shape[0] // 128):
        total_ref[0, j : j + 1, :] = to_lanes(total[j * 128 : (j + 1) * 128])


def student_pass(packet, stud, cols, cols_t):
    dp, _, width = packet.shape
    mine = cols.shape[1]
    return pl.pallas_call(
        student_kernel,
        grid=(dp,),
        in_specs=[
            pl.BlockSpec((1, stud, width), lambda i: (i, 0, 0)),
            pl.BlockSpec((width, mine), lambda i: (0, 0)),
            pl.BlockSpec((mine, width), lambda i: (0, 0)),
        ],
        out_specs=[
            pl.BlockSpec((stud, mine), lambda i: (i, 0)),
            pl.BlockSpec((stud, width), lambda i: (i, 0)),
            pl.BlockSpec((1, stud // 128, 128), lambda i: (i, 0, 0)),
            pl.BlockSpec((stud, width), lambda i: (i, 0)),
        ],
        out_shape=[
            jax.ShapeDtypeStruct((dp * stud, mine), jnp.bfloat16),
            jax.ShapeDtypeStruct((dp * stud, width), jnp.float32),
            jax.ShapeDtypeStruct((dp, stud // 128, 128), jnp.float32),
            jax.ShapeDtypeStruct((dp * stud, width), jnp.bfloat16),
        ],
        compiler_params=pltpu.CompilerParams(vmem_limit_bytes=52 * MIB),
        cost_estimate=pl.CostEstimate(
            flops=4 * dp * stud * mine * width, bytes_accessed=2 * dp * stud * mine, transcendentals=dp * stud * mine
        ),
        name="student_pass",
    )(packet, cols, cols_t)


def sinkhorn_kernel(
    dp, protos, rows_ref, cols_ref, part_ref, targets_ref, total_ref, expo, cols, near, far, near_sems, far_sems
):
    here = {"dp": lax.axis_index("dp"), "proto": lax.axis_index("proto")}
    sizes = {"dp": dp, "proto": protos}
    barrier = pltpu.get_barrier_semaphore()
    for axis, size in sizes.items():
        for k in range(1, size):
            pl.semaphore_signal(
                barrier,
                inc=1,
                device_id={axis: lax.rem(here[axis] + k, size)},
                device_id_type=pl.DeviceIdType.MESH,
            )
    count, mine = expo.shape
    blocks = count // 128

    def rows_at(block):
        return pl.ds(pl.multiple_of(block * 128, 128), 128)

    cols[...] = jnp.zeros_like(cols)

    @pl.loop(0, blocks)
    def _(block):
        at = rows_at(block)
        for start, step in chunks(mine):
            values = jnp.exp2(
                dot(rows_ref[at, :], cols_ref[:, start : start + step], 1, 0) * (LOG2E / teacher_temp)
            )
            expo[at, start : start + step] = values
            cols[:, start : start + step] += jnp.sum(values, axis=0, keepdims=True)

    pl.semaphore_wait(barrier, dp + protos - 2)

    def exchange(axis, buffer, sems, it, rows):
        copies = []
        for k in range(1, sizes[axis]):
            copy = pltpu.make_async_remote_copy(
                src_ref=buffer.at[it, 0, pl.ds(0, rows)],
                dst_ref=buffer.at[it, k, pl.ds(0, rows)],
                send_sem=sems.at[0, it, k],
                recv_sem=sems.at[1, it, k],
                device_id={axis: lax.rem(here[axis] + k, sizes[axis])},
                device_id_type=pl.DeviceIdType.MESH,
            )
            copy.start()
            copies.append(copy)
        for copy in copies:
            copy.wait()
        total = buffer[it, 0, 0:rows]
        for k in range(1, sizes[axis]):
            total = total + buffer[it, k, 0:rows]
        return total

    for it in range(ITERS):
        if it:
            cols[...] = jnp.zeros_like(cols)

            @pl.loop(0, blocks)
            def _(block):
                at = rows_at(block)
                scale = to_column(total_ref[pl.ds(block, 1), :])
                cols[...] += jnp.sum(expo[at, :] * scale, axis=0, keepdims=True)

        cols[...] = 1.0 / cols[...]

        @pl.loop(0, blocks)
        def _(block):
            sums = jnp.sum(expo[rows_at(block), :] * cols[...], axis=1, keepdims=True)
            near[it, 0, pl.ds(block, 1), :] = to_lanes(sums)

        used = blocks
        if it == 0:
            used = near.shape[2]
            near[0, 0, blocks:used, :] = part_ref[...]
        far[it, 0, 0:used] = exchange("proto", near, near_sems, it, used)
        total = exchange("dp", far, far_sems, it, used)
        total_ref[0:blocks, :] = 1.0 / total[0:blocks]
        if it == 0:
            total_ref[blocks:used, :] = total[blocks:used]

    @pl.loop(0, blocks)
    def _(block):
        at = rows_at(block)
        scale = to_column(total_ref[pl.ds(block, 1), :])
        targets_ref[at, :] = (expo[at, :] * scale * cols[...]).astype(jnp.bfloat16)


def sinkhorn(dp, protos, rows, cols, part):
    count, mine = rows.shape[0], cols.shape[1]
    used = count // 128 + part.shape[0]
    vmem = pl.BlockSpec(memory_space=pltpu.VMEM)
    targets, total = pl.pallas_call(
        functools.partial(sinkhorn_kernel, dp, protos),
        in_specs=[vmem] * 3,
        out_specs=[vmem] * 2,
        out_shape=[
            jax.ShapeDtypeStruct((count, mine), jnp.bfloat16),
            jax.ShapeDtypeStruct((used, 128), jnp.float32),
        ],
        scratch_shapes=[
            pltpu.VMEM((count, mine), jnp.float32),
            pltpu.VMEM((1, mine), jnp.float32),
            pltpu.VMEM((ITERS, protos, used, 128), jnp.float32),
            pltpu.VMEM((ITERS, dp, used, 128), jnp.float32),
            pltpu.SemaphoreType.DMA((2, ITERS, protos)),
            pltpu.SemaphoreType.DMA((2, ITERS, dp)),
        ],
        compiler_params=pltpu.CompilerParams(
            collective_id=1, has_side_effects=True, vmem_limit_bytes=52 * MIB
        ),
        cost_estimate=pl.CostEstimate(
            flops=2 * count * mine * rows.shape[1], bytes_accessed=4 * count * mine, transcendentals=count * mine
        ),
        name="sinkhorn",
    )(rows, cols, part)
    return targets, total[count // 128 :]


def body(teacher_feat, student_feat, teacher_weight, head_weight, pairing):
    dp, me = lax.axis_size("dp"), lax.axis_index("dp")
    protos = lax.axis_size("proto")
    teach, width = teacher_feat.shape
    stud = student_feat.shape[0]
    images = teach // 2
    crops = stud // images
    mine = head_weight.shape[1] // dp
    scale = 1.0 / (student_temp * stud * dp)

    teach_unit = unit_rows(teacher_feat)[0]
    stud_unit, stud_inverse = unit_rows(student_feat)
    view = (pairing - me * teach) // images
    kept = stud_unit.astype(jnp.bfloat16).astype(jnp.float32).reshape(crops, images, width)
    second = (view == 1).reshape(crops, images, 1)
    pair_sums = jnp.concatenate(
        [jnp.sum(jnp.where(second, 0.0, kept), 0), jnp.sum(jnp.where(second, kept, 0.0), 0)], 0
    )
    packet = jnp.concatenate([stud_unit, teach_unit, pair_sums], 0)
    packet = lax.optimization_barrier(lax.all_gather(packet, "dp", axis=0, tiled=False))
    teach_rows = packet[:, stud : stud + teach].reshape(dp * teach, width).astype(jnp.bfloat16)
    sums = packet[:, stud + teach :].reshape(dp * teach, width)

    teach_cols = unit_columns(lax.dynamic_slice_in_dim(teacher_weight, me * mine, mine, 1))[0].astype(jnp.bfloat16)
    head_unit, head_inverse = unit_columns(lax.dynamic_slice_in_dim(head_weight, me * mine, mine, 1))
    head_cols = head_unit.astype(jnp.bfloat16)

    expo_s, raw, part, stud_rows = student_pass(packet, stud, head_cols, head_cols.T)
    raw = lax.psum_scatter(raw.reshape(dp, stud, width), "dp", scatter_dimension=0, tiled=False)
    raw = lax.psum_scatter(raw, "proto", scatter_dimension=1, tiled=True)
    targets, totals = sinkhorn(dp, protos, teach_rows, teach_cols, part.reshape(dp * stud // 128, 128))
    totals = totals.reshape(dp, stud)

    aim = dot(targets, head_cols, 1, 1).reshape(dp, teach, width)
    aim = lax.psum_scatter(aim, "dp", scatter_dimension=0, tiled=False)
    aim = lax.psum_scatter(aim, "proto", scatter_dimension=1, tiled=True)
    share = width // protos
    offset = lax.axis_index("proto") * share
    aims = aim.reshape(2, 1, images, share)
    picked = jnp.where(second, aims[1], aims[0]).reshape(stud, share)
    own_part = (raw / lax.dynamic_index_in_dim(totals, me, 0, False)[:, None] - picked) * scale
    own_unit = lax.dynamic_slice_in_dim(stud_unit, offset, share, 1)
    along = lax.psum(jnp.sum(own_unit * own_part, axis=1), "proto")
    student_grad = (own_part - own_unit * along[:, None]) * stud_inverse

    scaled = (stud_rows.astype(jnp.float32) / totals.reshape(dp * stud, 1)).astype(jnp.bfloat16)
    high, low = split_sum(sums)
    weight_grad = (dot(scaled, expo_s, 0, 0) - dot(high, targets, 0, 0) - dot(low, targets, 0, 0)) * scale
    inner = jnp.sum(head_unit * weight_grad, axis=0, keepdims=True)
    head_grad = (weight_grad - head_unit * inner) * head_inverse
    head_grad = lax.all_to_all(head_grad, "dp", split_axis=0, concat_axis=1, tiled=True)
    return (student_grad, head_grad)


def solution(mesh):
    return jax.shard_map(
        body,
        mesh=mesh,
        in_specs=(P("dp", None), P("dp", None), P(None, "proto"), P(None, "proto"), P("dp")),
        out_specs=(P("dp", "proto"), P("dp", "proto")),
        check_vma=False,
    )
```

```python
import functools
import math

import jax
import jax.numpy as jnp
from jax import lax
from jax.experimental import pallas as pl
from jax.experimental.pallas import tpu as pltpu
from jax.sharding import PartitionSpec as P

ITERS = 3


tiny_eps = 1e-06
teacher_temp = 0.04
student_temp = 0.1
BOTH = ("dp", "proto")


def unit_rows(values):
    floats = values.astype(jnp.float32)
    inverse = lax.rsqrt(jnp.sum(floats * floats, axis=1, keepdims=True) + tiny_eps)
    return (floats * inverse, inverse)


def unit_columns(values):
    floats = values.astype(jnp.float32)
    inverse = lax.rsqrt(jnp.sum(floats * floats, axis=0, keepdims=True) + tiny_eps)
    return (floats * inverse, inverse)


def dot(a, b, da, db):
    return lax.dot_general(a, b, (((da,), (db,)), ((), ())), preferred_element_type=jnp.float32)


def split_sum(values):
    high = values.astype(jnp.bfloat16)
    return high, (values - high.astype(jnp.float32)).astype(jnp.bfloat16)


LOG2E = math.log2(math.e)
MIB = 1 << 20


def diagonal():
    shape = (128, 128)
    return lax.broadcasted_iota(jnp.int32, shape, 0) == lax.broadcasted_iota(jnp.int32, shape, 1)


def to_lanes(column):
    return jnp.sum(jnp.where(diagonal(), column, 0.0), axis=0, keepdims=True)


def to_column(lanes):
    return jnp.sum(jnp.where(diagonal(), lanes, 0.0), axis=1, keepdims=True)


def chunks(size):
    step = min(size, 1024)
    return [(c, step) for c in range(0, size, step)]


def student_kernel(rows_ref, cols_ref, cols_t_ref, expo_ref, raw_ref, total_ref, kept_ref):
    rows = rows_ref[0].astype(jnp.bfloat16)
    kept_ref[...] = rows
    raw, total = None, None
    for start, step in chunks(cols_ref.shape[1]):
        logits = dot(rows, cols_ref[:, start : start + step], 1, 0)
        expo = jnp.exp2(logits * (LOG2E / student_temp))
        part = jnp.sum(expo, axis=1, keepdims=True)
        kept = expo.astype(jnp.bfloat16)
        expo_ref[:, start : start + step] = kept
        grad = dot(kept, cols_t_ref[start : start + step, :], 1, 0)
        total = part if total is None else total + part
        raw = grad if raw is None else raw + grad
    raw_ref[...] = raw.T
    for j in range(rows.shape[0] // 128):
        total_ref[0, j : j + 1, :] = to_lanes(total[j * 128 : (j + 1) * 128])


def student_pass(packet, stud, cols, cols_t):
    dp, _, width = packet.shape
    mine = cols.shape[1]
    return pl.pallas_call(
        student_kernel,
        grid=(dp,),
        in_specs=[
            pl.BlockSpec((1, stud, width), lambda i: (i, 0, 0)),
            pl.BlockSpec((width, mine), lambda i: (0, 0)),
            pl.BlockSpec((mine, width), lambda i: (0, 0)),
        ],
        out_specs=[
            pl.BlockSpec((stud, mine), lambda i: (i, 0)),
            pl.BlockSpec((width, stud), lambda i: (0, i)),
            pl.BlockSpec((1, stud // 128, 128), lambda i: (i, 0, 0)),
            pl.BlockSpec((stud, width), lambda i: (i, 0)),
        ],
        out_shape=[
            jax.ShapeDtypeStruct((dp * stud, mine), jnp.bfloat16),
            jax.ShapeDtypeStruct((width, dp * stud), jnp.float32),
            jax.ShapeDtypeStruct((dp, stud // 128, 128), jnp.float32),
            jax.ShapeDtypeStruct((dp * stud, width), jnp.bfloat16),
        ],
        compiler_params=pltpu.CompilerParams(vmem_limit_bytes=52 * MIB),
        cost_estimate=pl.CostEstimate(
            flops=4 * dp * stud * mine * width, bytes_accessed=2 * dp * stud * mine, transcendentals=dp * stud * mine
        ),
        name="student_pass",
    )(packet, cols, cols_t)


def positions():
    return {"dp": lax.axis_index("dp"), "proto": lax.axis_index("proto")}


def greet(here, sizes):
    barrier = pltpu.get_barrier_semaphore()
    for axis, size in sizes.items():
        for k in range(1, size):
            pl.semaphore_signal(
                barrier,
                inc=1,
                device_id={axis: lax.rem(here[axis] + k, size)},
                device_id_type=pl.DeviceIdType.MESH,
            )
    pl.semaphore_wait(barrier, sum(sizes.values()) - len(sizes))


def sends(here, sizes, axis, source, target, sems):
    copies = []
    for k in range(1, sizes[axis]):
        peer = lax.rem(here[axis] + k, sizes[axis])
        copies.append(
            pltpu.make_async_remote_copy(
                src_ref=source(peer),
                dst_ref=target(k),
                send_sem=sems.at[0, k],
                recv_sem=sems.at[1, k],
                device_id={axis: peer},
                device_id_type=pl.DeviceIdType.MESH,
            )
        )
    return copies


def start_all(copies):
    for copy in copies:
        copy.start()
    return copies


def wait_all(copies):
    for copy in copies:
        copy.wait()


def sinkhorn_kernel(
    dp,
    protos,
    rows_ref,
    cols_ref,
    part_ref,
    raw_ref,
    targets_ref,
    total_ref,
    raw_sum_ref,
    expo,
    cols,
    near,
    far,
    raw_in,
    near_sems,
    far_sems,
    raw_sems,
):
    here, sizes = positions(), {"dp": dp, "proto": protos}
    greet(here, sizes)
    share = raw_sum_ref.shape[0]

    def part_of(peer):
        return pl.ds(pl.multiple_of(peer * share, 8), share)

    raw_copies = start_all(
        sends(here, sizes, "proto", lambda peer: raw_ref.at[part_of(peer)], lambda k: raw_in.at[k], raw_sems)
    )
    count, mine = expo.shape
    blocks = count // 128

    def rows_at(block):
        return pl.ds(pl.multiple_of(block * 128, 128), 128)

    cols[...] = jnp.zeros_like(cols)

    @pl.loop(0, blocks)
    def _(block):
        at = rows_at(block)
        for start, step in chunks(mine):
            values = jnp.exp2(
                dot(rows_ref[at, :], cols_ref[:, start : start + step], 1, 0) * (LOG2E / teacher_temp)
            )
            expo[at, start : start + step] = values
            cols[:, start : start + step] += jnp.sum(values, axis=0, keepdims=True)

    def exchange(axis, buffer, sems, it, rows):
        wait_all(
            start_all(
                sends(
                    here,
                    sizes,
                    axis,
                    lambda peer: buffer.at[it, 0, pl.ds(0, rows)],
                    lambda k: buffer.at[it, k, pl.ds(0, rows)],
                    sems.at[it],
                )
            )
        )
        total = buffer[it, 0, 0:rows]
        for k in range(1, sizes[axis]):
            total = total + buffer[it, k, 0:rows]
        return total

    for it in range(ITERS):
        if it:
            cols[...] = jnp.zeros_like(cols)

            @pl.loop(0, blocks)
            def _(block):
                at = rows_at(block)
                scale = to_column(total_ref[pl.ds(block, 1), :])
                cols[...] += jnp.sum(expo[at, :] * scale, axis=0, keepdims=True)

        cols[...] = 1.0 / cols[...]

        @pl.loop(0, blocks)
        def _(block):
            sums = jnp.sum(expo[rows_at(block), :] * cols[...], axis=1, keepdims=True)
            near[it, 0, pl.ds(block, 1), :] = to_lanes(sums)

        used = blocks
        if it == 0:
            used = near.shape[2]
            near[0, 0, blocks:used, :] = part_ref[...]
        far[it, 0, 0:used] = exchange("proto", near, near_sems, it, used)
        total = exchange("dp", far, far_sems, it, used)
        total_ref[0:blocks, :] = 1.0 / total[0:blocks]
        if it == 0:
            total_ref[blocks:used, :] = total[blocks:used]

    @pl.loop(0, blocks)
    def _(block):
        at = rows_at(block)
        scale = to_column(total_ref[pl.ds(block, 1), :])
        targets_ref[at, :] = (expo[at, :] * scale * cols[...]).astype(jnp.bfloat16)

    wait_all(raw_copies)
    total = raw_ref[part_of(here["proto"]), :]
    for k in range(1, protos):
        total = total + raw_in[k]
    raw_sum_ref[...] = total


def sinkhorn(dp, protos, rows, cols, part, raw):
    count, mine = rows.shape[0], cols.shape[1]
    used = count // 128 + part.shape[0]
    vmem = pl.BlockSpec(memory_space=pltpu.VMEM)
    share = raw.shape[0] // protos
    targets, total, raw_sum = pl.pallas_call(
        functools.partial(sinkhorn_kernel, dp, protos),
        in_specs=[vmem] * 4,
        out_specs=[vmem] * 3,
        out_shape=[
            jax.ShapeDtypeStruct((count, mine), jnp.bfloat16),
            jax.ShapeDtypeStruct((used, 128), jnp.float32),
            jax.ShapeDtypeStruct((share, raw.shape[1]), jnp.float32),
        ],
        scratch_shapes=[
            pltpu.VMEM((count, mine), jnp.float32),
            pltpu.VMEM((1, mine), jnp.float32),
            pltpu.VMEM((ITERS, protos, used, 128), jnp.float32),
            pltpu.VMEM((ITERS, dp, used, 128), jnp.float32),
            pltpu.VMEM((protos, share, raw.shape[1]), jnp.float32),
            pltpu.SemaphoreType.DMA((ITERS, 2, protos)),
            pltpu.SemaphoreType.DMA((ITERS, 2, dp)),
            pltpu.SemaphoreType.DMA((2, protos)),
        ],
        compiler_params=pltpu.CompilerParams(
            collective_id=1, has_side_effects=True, vmem_limit_bytes=52 * MIB
        ),
        cost_estimate=pl.CostEstimate(
            flops=2 * count * mine * rows.shape[1], bytes_accessed=4 * count * mine, transcendentals=count * mine
        ),
        name="sinkhorn",
    )(rows, cols, part, raw)
    return targets, total[count // 128 :], raw_sum


def weight_kernel(
    dp,
    protos,
    steps,
    scale,
    expo_ref,
    targets_ref,
    head_ref,
    rows_ref,
    high_ref,
    low_ref,
    raw_ref,
    aim_ref,
    grad_ref,
    raw_own_ref,
    aim_own_ref,
    stage,
    raw_in,
    aim_near,
    aim_sum,
    aim_far,
    grad_sems,
    own_sem,
    raw_sems,
    near_sems,
    far_sems,
):
    here, sizes = positions(), {"dp": dp, "proto": protos}
    step = pl.program_id(0)
    share, stud = raw_own_ref.shape
    teach = aim_own_ref.shape[1]
    mine = stage.shape[1]
    size = head_ref.shape[1]
    depth = stage.shape[0] // dp

    def band(peer, height):
        return pl.ds(pl.multiple_of(peer * height, 8), height)

    def lanes(peer, length):
        return pl.ds(pl.multiple_of(peer * length, 128), length)

    raw_copies = sends(here, sizes, "dp", lambda e: raw_ref.at[:, lanes(e, stud)], lambda k: raw_in.at[k], raw_sems)
    near_copies = sends(here, sizes, "proto", lambda e: aim_ref.at[band(e, share)], lambda k: aim_near.at[k], near_sems)
    far_copies = sends(here, sizes, "dp", lambda e: aim_sum.at[:, lanes(e, teach)], lambda k: aim_far.at[k], far_sems)

    def columns(j):
        return pl.ds(pl.multiple_of(here["dp"] * mine + j * size, 128), size)

    def grad_copies(j):
        local = pl.ds(pl.multiple_of(j * size, 128), size)
        return sends(
            here,
            sizes,
            "dp",
            lambda e: stage.at[band(e, depth), local],
            lambda k: grad_ref.at[:, columns(j)],
            grad_sems.at[j],
        )

    @pl.when(step == 0)
    def _():
        greet(here, sizes)
        start_all(near_copies)
        start_all(raw_copies)

    targets = targets_ref[...]
    grad = dot(rows_ref[...], expo_ref[...], 1, 0) - dot(high_ref[...], targets, 1, 0) - dot(low_ref[...], targets, 1, 0)
    grad = grad * scale
    unit, inverse = unit_columns(head_ref[...])
    inner = jnp.sum(unit * grad, axis=0, keepdims=True)
    stage[:, pl.ds(pl.multiple_of(step * size, 128), size)] = (grad - unit * inner) * inverse
    start_all(grad_copies(step))

    @pl.when(step == steps - 1)
    def _():
        own = pltpu.make_async_copy(
            stage.at[band(here["dp"], depth)],
            grad_ref.at[:, pl.ds(pl.multiple_of(here["dp"] * mine, 128), mine)],
            own_sem,
        )
        own.start()
        wait_all(near_copies)
        total = aim_ref[band(here["proto"], share), :]
        for k in range(1, protos):
            total = total + aim_near[k]
        aim_sum[...] = total
        start_all(far_copies)
        wait_all(raw_copies)
        total = raw_ref[:, lanes(here["dp"], stud)]
        for k in range(1, dp):
            total = total + raw_in[k]
        raw_own_ref[...] = total
        wait_all(far_copies)
        total = aim_sum[:, lanes(here["dp"], teach)]
        for k in range(1, dp):
            total = total + aim_far[k]
        aim_own_ref[...] = total
        own.wait()
        for j in range(steps):
            wait_all(grad_copies(j))


def weight_pass(dp, protos, scale, expo, targets, head, rows, high, low, raw, aim):
    width, mine = head.shape
    count, teach = rows.shape[1], high.shape[1]
    size = min(mine, 512)
    steps = mine // size
    share = raw.shape[0]

    def whole(array):
        return pl.BlockSpec(array.shape, lambda i: (0, 0))

    def block(array):
        return pl.BlockSpec((array.shape[0], size), lambda i: (0, i))

    own = [(share, count // dp), (share, teach // dp)]
    return pl.pallas_call(
        functools.partial(weight_kernel, dp, protos, steps, scale),
        grid=(steps,),
        in_specs=[block(expo), block(targets), block(head)] + [whole(x) for x in (rows, high, low, raw, aim)],
        out_specs=[pl.BlockSpec(memory_space=pl.ANY)] + [pl.BlockSpec(shape, lambda i: (0, 0)) for shape in own],
        out_shape=[jax.ShapeDtypeStruct(shape, jnp.float32) for shape in [(width // dp, dp * mine)] + own],
        scratch_shapes=[
            pltpu.VMEM((width, mine), jnp.float32),
            pltpu.VMEM((dp,) + own[0], jnp.float32),
            pltpu.VMEM((protos, share, teach), jnp.float32),
            pltpu.VMEM((share, teach), jnp.float32),
            pltpu.VMEM((dp,) + own[1], jnp.float32),
            pltpu.SemaphoreType.DMA((steps, 2, dp)),
            pltpu.SemaphoreType.DMA,
            pltpu.SemaphoreType.DMA((2, dp)),
            pltpu.SemaphoreType.DMA((2, protos)),
            pltpu.SemaphoreType.DMA((2, dp)),
        ],
        compiler_params=pltpu.CompilerParams(
            collective_id=2, has_side_effects=True, vmem_limit_bytes=52 * MIB
        ),
        cost_estimate=pl.CostEstimate(
            flops=2 * count * mine * width, bytes_accessed=2 * count * mine, transcendentals=0
        ),
        name="weight_pass",
    )(expo, targets, head, rows, high, low, raw, aim)


def body(teacher_feat, student_feat, teacher_weight, head_weight, pairing):
    dp, me = lax.axis_size("dp"), lax.axis_index("dp")
    protos = lax.axis_size("proto")
    teach, width = teacher_feat.shape
    stud = student_feat.shape[0]
    images = teach // 2
    crops = stud // images
    mine = head_weight.shape[1] // dp
    scale = 1.0 / (student_temp * stud * dp)

    teach_unit = unit_rows(teacher_feat)[0]
    stud_unit, stud_inverse = unit_rows(student_feat)
    view = (pairing - me * teach) // images
    kept = stud_unit.astype(jnp.bfloat16).astype(jnp.float32).reshape(crops, images, width)
    second = (view == 1).reshape(crops, images, 1)
    pair_sums = jnp.concatenate(
        [jnp.sum(jnp.where(second, 0.0, kept), 0), jnp.sum(jnp.where(second, kept, 0.0), 0)], 0
    )
    packet = jnp.concatenate([stud_unit, teach_unit, pair_sums], 0)
    packet = lax.optimization_barrier(lax.all_gather(packet, "dp", axis=0, tiled=False))
    teach_rows = packet[:, stud : stud + teach].reshape(dp * teach, width).astype(jnp.bfloat16)
    sums = packet[:, stud + teach :].reshape(dp * teach, width)

    teach_cols = unit_columns(lax.dynamic_slice_in_dim(teacher_weight, me * mine, mine, 1))[0].astype(jnp.bfloat16)
    own_head = lax.dynamic_slice_in_dim(head_weight, me * mine, mine, 1)
    head_cols = unit_columns(own_head)[0].astype(jnp.bfloat16)

    expo_s, raw, part, stud_rows = student_pass(packet, stud, head_cols, head_cols.T)
    targets, totals, raw = sinkhorn(
        dp, protos, teach_rows, teach_cols, part.reshape(dp * stud // 128, 128), raw
    )
    totals = totals.reshape(dp, stud)
    aim = dot(head_cols, targets, 1, 1)
    scaled = (stud_rows.astype(jnp.float32) / totals.reshape(dp * stud, 1)).astype(jnp.bfloat16)
    high, low = split_sum(sums.T)
    head_grad, raw, aim = weight_pass(
        dp, protos, scale, expo_s, targets, own_head, scaled.T, high, low, raw, aim
    )

    share = width // protos
    offset = lax.axis_index("proto") * share
    view_lanes = (view == 1).reshape(1, crops, images)
    aims = aim.reshape(share, 2, 1, images)
    picked = jnp.where(view_lanes, aims[:, 1], aims[:, 0]).reshape(share, stud)
    own_part = (raw / lax.dynamic_index_in_dim(totals, me, 0, True) - picked) * scale
    own_unit = lax.dynamic_slice_in_dim(stud_unit, offset, share, 1).T
    along = lax.psum(jnp.sum(own_unit * own_part, axis=0, keepdims=True), "proto")
    student_grad = (own_part - own_unit * along).T * stud_inverse
    return (student_grad, head_grad)


def solution(mesh):
    return jax.shard_map(
        body,
        mesh=mesh,
        in_specs=(P("dp", None), P("dp", None), P(None, "proto"), P(None, "proto"), P("dp")),
        out_specs=(P("dp", "proto"), P("dp", "proto")),
        check_vma=False,
    )
```

```python
import functools
import math

import jax
import jax.numpy as jnp
from jax import lax
from jax.experimental import pallas as pl
from jax.experimental.pallas import tpu as pltpu
from jax.sharding import PartitionSpec as P

ITERS = 3


tiny_eps = 1e-06
teacher_temp = 0.04
student_temp = 0.1
BOTH = ("dp", "proto")


def unit_rows(values):
    floats = values.astype(jnp.float32)
    inverse = lax.rsqrt(jnp.sum(floats * floats, axis=1, keepdims=True) + tiny_eps)
    return (floats * inverse, inverse)


def unit_columns(values):
    floats = values.astype(jnp.float32)
    inverse = lax.rsqrt(jnp.sum(floats * floats, axis=0, keepdims=True) + tiny_eps)
    return (floats * inverse, inverse)


def dot(a, b, da, db):
    return lax.dot_general(a, b, (((da,), (db,)), ((), ())), preferred_element_type=jnp.float32)


def split_sum(values):
    high = values.astype(jnp.bfloat16)
    return high, (values - high.astype(jnp.float32)).astype(jnp.bfloat16)


LOG2E = math.log2(math.e)
MIB = 1 << 20


def diagonal():
    shape = (128, 128)
    return lax.broadcasted_iota(jnp.int32, shape, 0) == lax.broadcasted_iota(jnp.int32, shape, 1)


def to_lanes(column):
    return jnp.sum(jnp.where(diagonal(), column, 0.0), axis=0, keepdims=True)


def to_column(lanes):
    return jnp.sum(jnp.where(diagonal(), lanes, 0.0), axis=1, keepdims=True)


def chunks(size):
    step = min(size, 1024)
    return [(c, step) for c in range(0, size, step)]


def student_kernel(
    rows_ref,
    teach_ref,
    sums_ref,
    cols_ref,
    cols_t_ref,
    expo_ref,
    raw_ref,
    total_ref,
    kept_ref,
    teach_rows_ref,
    high_ref,
    low_ref,
):
    rows = rows_ref[0].astype(jnp.bfloat16)
    kept_ref[...] = rows_ref[0].T.astype(jnp.bfloat16)
    teach_rows_ref[...] = teach_ref[0].astype(jnp.bfloat16)
    high_ref[...], low_ref[...] = split_sum(sums_ref[0].T)
    raw, total = None, None
    for start, step in chunks(cols_ref.shape[1]):
        logits = dot(rows, cols_ref[:, start : start + step], 1, 0)
        expo = jnp.exp2(logits * (LOG2E / student_temp))
        part = jnp.sum(expo, axis=1, keepdims=True)
        kept = expo.astype(jnp.bfloat16)
        expo_ref[:, start : start + step] = kept
        grad = dot(kept, cols_t_ref[start : start + step, :], 1, 0)
        total = part if total is None else total + part
        raw = grad if raw is None else raw + grad
    raw_ref[...] = raw.T
    for j in range(rows.shape[0] // 128):
        total_ref[0, j : j + 1, :] = to_lanes(total[j * 128 : (j + 1) * 128])


def student_pass(packet, stud, teach, cols, cols_t):
    dp, _, width = packet.shape
    first = stud // teach
    assert stud == first * teach
    mine = cols.shape[1]
    return pl.pallas_call(
        student_kernel,
        grid=(dp,),
        in_specs=[
            pl.BlockSpec((1, stud, width), lambda i: (i, 0, 0)),
            pl.BlockSpec((1, teach, width), lambda i: (i, first, 0)),
            pl.BlockSpec((1, teach, width), lambda i: (i, first + 1, 0)),
            pl.BlockSpec((width, mine), lambda i: (0, 0)),
            pl.BlockSpec((mine, width), lambda i: (0, 0)),
        ],
        out_specs=[
            pl.BlockSpec((stud, mine), lambda i: (i, 0)),
            pl.BlockSpec((width, stud), lambda i: (0, i)),
            pl.BlockSpec((1, stud // 128, 128), lambda i: (i, 0, 0)),
            pl.BlockSpec((width, stud), lambda i: (0, i)),
            pl.BlockSpec((teach, width), lambda i: (i, 0)),
            pl.BlockSpec((width, teach), lambda i: (0, i)),
            pl.BlockSpec((width, teach), lambda i: (0, i)),
        ],
        out_shape=[
            jax.ShapeDtypeStruct((dp * stud, mine), jnp.bfloat16),
            jax.ShapeDtypeStruct((width, dp * stud), jnp.float32),
            jax.ShapeDtypeStruct((dp, stud // 128, 128), jnp.float32),
            jax.ShapeDtypeStruct((width, dp * stud), jnp.bfloat16),
            jax.ShapeDtypeStruct((dp * teach, width), jnp.bfloat16),
            jax.ShapeDtypeStruct((width, dp * teach), jnp.bfloat16),
            jax.ShapeDtypeStruct((width, dp * teach), jnp.bfloat16),
        ],
        compiler_params=pltpu.CompilerParams(vmem_limit_bytes=52 * MIB),
        cost_estimate=pl.CostEstimate(
            flops=4 * dp * stud * mine * width, bytes_accessed=2 * dp * stud * mine, transcendentals=dp * stud * mine
        ),
        name="student_pass",
    )(packet, packet, packet, cols, cols_t)


def positions():
    return {"dp": lax.axis_index("dp"), "proto": lax.axis_index("proto")}


def greet(here, sizes):
    barrier = pltpu.get_barrier_semaphore()
    for axis, size in sizes.items():
        for k in range(1, size):
            pl.semaphore_signal(
                barrier,
                inc=1,
                device_id={axis: lax.rem(here[axis] + k, size)},
                device_id_type=pl.DeviceIdType.MESH,
            )
    pl.semaphore_wait(barrier, sum(sizes.values()) - len(sizes))


def sends(here, sizes, axis, source, target, sems):
    copies = []
    for k in range(1, sizes[axis]):
        peer = lax.rem(here[axis] + k, sizes[axis])
        copies.append(
            pltpu.make_async_remote_copy(
                src_ref=source(peer),
                dst_ref=target(k),
                send_sem=sems.at[0, k],
                recv_sem=sems.at[1, k],
                device_id={axis: peer},
                device_id_type=pl.DeviceIdType.MESH,
            )
        )
    return copies


def start_all(copies):
    for copy in copies:
        copy.start()
    return copies


def wait_all(copies):
    for copy in copies:
        copy.wait()


def sinkhorn_kernel(
    dp,
    protos,
    rows_ref,
    cols_ref,
    part_ref,
    targets_ref,
    total_ref,
    expo,
    cols,
    near,
    far,
    near_sems,
    far_sems,
):
    here, sizes = positions(), {"dp": dp, "proto": protos}
    greet(here, sizes)
    count, mine = expo.shape
    blocks = count // 128

    def rows_at(block):
        return pl.ds(pl.multiple_of(block * 128, 128), 128)

    cols[...] = jnp.zeros_like(cols)

    @pl.loop(0, blocks)
    def _(block):
        at = rows_at(block)
        for start, step in chunks(mine):
            values = jnp.exp2(
                dot(rows_ref[at, :], cols_ref[:, start : start + step], 1, 0) * (LOG2E / teacher_temp)
            )
            expo[at, start : start + step] = values
            cols[:, start : start + step] += jnp.sum(values, axis=0, keepdims=True)

    def exchange(axis, buffer, sems, it, rows):
        wait_all(
            start_all(
                sends(
                    here,
                    sizes,
                    axis,
                    lambda peer: buffer.at[it, 0, pl.ds(0, rows)],
                    lambda k: buffer.at[it, k, pl.ds(0, rows)],
                    sems.at[it],
                )
            )
        )
        total = buffer[it, 0, 0:rows]
        for k in range(1, sizes[axis]):
            total = total + buffer[it, k, 0:rows]
        return total

    for it in range(ITERS):
        if it:
            cols[...] = jnp.zeros_like(cols)

            @pl.loop(0, blocks)
            def _(block):
                at = rows_at(block)
                scale = to_column(total_ref[pl.ds(block, 1), :])
                cols[...] += jnp.sum(expo[at, :] * scale, axis=0, keepdims=True)

        cols[...] = 1.0 / cols[...]

        @pl.loop(0, blocks)
        def _(block):
            sums = jnp.sum(expo[rows_at(block), :] * cols[...], axis=1, keepdims=True)
            near[it, 0, pl.ds(block, 1), :] = to_lanes(sums)

        used = blocks
        if it == 0:
            used = near.shape[2]
            near[0, 0, blocks:used, :] = part_ref[...]
        far[it, 0, 0:used] = exchange("proto", near, near_sems, it, used)
        total = exchange("dp", far, far_sems, it, used)
        total_ref[0:blocks, :] = 1.0 / total[0:blocks]
        if it == 0:
            total_ref[blocks:used, :] = total[blocks:used]

    @pl.loop(0, blocks)
    def _(block):
        at = rows_at(block)
        scale = to_column(total_ref[pl.ds(block, 1), :])
        targets_ref[at, :] = (expo[at, :] * scale * cols[...]).astype(jnp.bfloat16)


def sinkhorn(dp, protos, rows, cols, part):
    count, mine = rows.shape[0], cols.shape[1]
    used = count // 128 + part.shape[0]
    vmem = pl.BlockSpec(memory_space=pltpu.VMEM)
    targets, total = pl.pallas_call(
        functools.partial(sinkhorn_kernel, dp, protos),
        in_specs=[vmem] * 3,
        out_specs=[vmem] * 2,
        out_shape=[
            jax.ShapeDtypeStruct((count, mine), jnp.bfloat16),
            jax.ShapeDtypeStruct((used, 128), jnp.float32),
        ],
        scratch_shapes=[
            pltpu.VMEM((count, mine), jnp.float32),
            pltpu.VMEM((1, mine), jnp.float32),
            pltpu.VMEM((ITERS, protos, used, 128), jnp.float32),
            pltpu.VMEM((ITERS, dp, used, 128), jnp.float32),
            pltpu.SemaphoreType.DMA((ITERS, 2, protos)),
            pltpu.SemaphoreType.DMA((ITERS, 2, dp)),
        ],
        compiler_params=pltpu.CompilerParams(
            collective_id=1, has_side_effects=True, vmem_limit_bytes=52 * MIB
        ),
        cost_estimate=pl.CostEstimate(
            flops=2 * count * mine * rows.shape[1], bytes_accessed=4 * count * mine, transcendentals=count * mine
        ),
        name="sinkhorn",
    )(rows, cols, part)
    return targets, total[count // 128 :]


def weight_kernel(
    dp,
    protos,
    steps,
    scale,
    expo_ref,
    targets_ref,
    head_ref,
    rows_ref,
    high_ref,
    low_ref,
    raw_ref,
    aim_ref,
    grad_ref,
    raw_own_ref,
    aim_own_ref,
    stage,
    raw_near,
    raw_sum,
    raw_far,
    aim_near,
    aim_sum,
    aim_far,
    grad_sems,
    own_sem,
    raw_near_sems,
    raw_far_sems,
    near_sems,
    far_sems,
):
    here, sizes = positions(), {"dp": dp, "proto": protos}
    step = pl.program_id(0)
    share, stud = raw_own_ref.shape
    teach = aim_own_ref.shape[1]
    mine = stage.shape[1]
    size = head_ref.shape[1]
    depth = stage.shape[0] // dp

    def band(peer, height):
        return pl.ds(pl.multiple_of(peer * height, 8), height)

    def lanes(peer, length):
        return pl.ds(pl.multiple_of(peer * length, 128), length)

    raw_copies = sends(
        here, sizes, "dp", lambda e: raw_sum.at[:, lanes(e, stud)], lambda k: raw_far.at[k], raw_far_sems
    )
    each = dp // steps

    def block_copies(j):
        at = pl.ds(pl.multiple_of(j * each * stud, 128), each * stud)
        return sends(
            here,
            sizes,
            "proto",
            lambda e: raw_ref.at[band(e, share), at],
            lambda k: raw_near.at[k, :, at],
            raw_near_sems.at[j],
        )

    near_copies = sends(here, sizes, "proto", lambda e: aim_ref.at[band(e, share)], lambda k: aim_near.at[k], near_sems)
    far_copies = sends(here, sizes, "dp", lambda e: aim_sum.at[:, lanes(e, teach)], lambda k: aim_far.at[k], far_sems)

    def columns(j):
        return pl.ds(pl.multiple_of(here["dp"] * mine + j * size, 128), size)

    def grad_copies(j):
        local = pl.ds(pl.multiple_of(j * size, 128), size)
        return sends(
            here,
            sizes,
            "dp",
            lambda e: stage.at[band(e, depth), local],
            lambda k: grad_ref.at[:, columns(j)],
            grad_sems.at[j],
        )

    @pl.when(step == 0)
    def _():
        greet(here, sizes)
        start_all(near_copies)

    targets = targets_ref[...]
    grad = dot(rows_ref[...], expo_ref[...], 1, 0) - dot(high_ref[...], targets, 1, 0) - dot(low_ref[...], targets, 1, 0)
    grad = grad * scale
    unit, inverse = unit_columns(head_ref[...])
    inner = jnp.sum(unit * grad, axis=0, keepdims=True)
    stage[:, pl.ds(pl.multiple_of(step * size, 128), size)] = (grad - unit * inner) * inverse
    start_all(grad_copies(step))
    start_all(block_copies(step))

    @pl.when(step == steps - 1)
    def _():
        own = pltpu.make_async_copy(
            stage.at[band(here["dp"], depth)],
            grad_ref.at[:, pl.ds(pl.multiple_of(here["dp"] * mine, 128), mine)],
            own_sem,
        )
        own.start()
        wait_all(near_copies)
        total = aim_ref[band(here["proto"], share), :]
        for k in range(1, protos):
            total = total + aim_near[k]
        aim_sum[...] = total
        start_all(far_copies)
        for j in range(steps):
            wait_all(block_copies(j))
        total = raw_ref[band(here["proto"], share), :]
        for k in range(1, protos):
            total = total + raw_near[k]
        raw_sum[...] = total
        start_all(raw_copies)
        wait_all(raw_copies)
        total = raw_sum[:, lanes(here["dp"], stud)]
        for k in range(1, dp):
            total = total + raw_far[k]
        raw_own_ref[...] = total
        wait_all(far_copies)
        total = aim_sum[:, lanes(here["dp"], teach)]
        for k in range(1, dp):
            total = total + aim_far[k]
        aim_own_ref[...] = total
        own.wait()
        for j in range(steps):
            wait_all(grad_copies(j))


def weight_pass(dp, protos, scale, expo, targets, head, rows, high, low, raw, aim):
    width, mine = head.shape
    count, teach = rows.shape[1], high.shape[1]
    size = min(mine, 512)
    steps = mine // size
    assert dp % steps == 0
    share = width // protos

    def whole(array):
        return pl.BlockSpec(array.shape, lambda i: (0, 0))

    def block(array):
        return pl.BlockSpec((array.shape[0], size), lambda i: (0, i))

    own = [(share, count // dp), (share, teach // dp)]
    return pl.pallas_call(
        functools.partial(weight_kernel, dp, protos, steps, scale),
        grid=(steps,),
        in_specs=[block(expo), block(targets), block(head)]
        + [whole(x) for x in (rows, high, low)]
        + [pl.BlockSpec(memory_space=pltpu.VMEM)] * 2,
        out_specs=[pl.BlockSpec(memory_space=pl.ANY)] + [pl.BlockSpec(shape, lambda i: (0, 0)) for shape in own],
        out_shape=[jax.ShapeDtypeStruct(shape, jnp.float32) for shape in [(width // dp, dp * mine)] + own],
        scratch_shapes=[
            pltpu.VMEM((width, mine), jnp.float32),
            pltpu.VMEM((protos, share, count), jnp.float32),
            pltpu.VMEM((share, count), jnp.float32),
            pltpu.VMEM((dp,) + own[0], jnp.float32),
            pltpu.VMEM((protos, share, teach), jnp.float32),
            pltpu.VMEM((share, teach), jnp.float32),
            pltpu.VMEM((dp,) + own[1], jnp.float32),
            pltpu.SemaphoreType.DMA((steps, 2, dp)),
            pltpu.SemaphoreType.DMA,
            pltpu.SemaphoreType.DMA((steps, 2, protos)),
            pltpu.SemaphoreType.DMA((2, dp)),
            pltpu.SemaphoreType.DMA((2, protos)),
            pltpu.SemaphoreType.DMA((2, dp)),
        ],
        compiler_params=pltpu.CompilerParams(
            collective_id=2, has_side_effects=True, vmem_limit_bytes=52 * MIB
        ),
        cost_estimate=pl.CostEstimate(
            flops=2 * count * mine * width, bytes_accessed=2 * count * mine, transcendentals=0
        ),
        name="weight_pass",
    )(expo, targets, head, rows, high, low, raw, aim)


def body(teacher_feat, student_feat, teacher_weight, head_weight, pairing):
    dp, me = lax.axis_size("dp"), lax.axis_index("dp")
    protos = lax.axis_size("proto")
    teach, width = teacher_feat.shape
    stud = student_feat.shape[0]
    images = teach // 2
    crops = stud // images
    mine = head_weight.shape[1] // dp
    scale = 1.0 / (student_temp * stud * dp)

    teach_unit = unit_rows(teacher_feat)[0]
    stud_unit, stud_inverse = unit_rows(student_feat)
    view = (pairing - me * teach) // images
    kept = stud_unit.astype(jnp.bfloat16).astype(jnp.float32).reshape(crops, images, width)
    second = (view == 1).reshape(crops, images, 1)
    pair_sums = jnp.concatenate(
        [jnp.sum(jnp.where(second, 0.0, kept), 0), jnp.sum(jnp.where(second, kept, 0.0), 0)], 0
    )
    packet = jnp.concatenate([stud_unit, teach_unit, pair_sums], 0)
    packet = lax.all_gather(packet, "dp", axis=0, tiled=False)
    teach_cols = unit_columns(lax.dynamic_slice_in_dim(teacher_weight, me * mine, mine, 1))[0].astype(jnp.bfloat16)
    own_head = lax.dynamic_slice_in_dim(head_weight, me * mine, mine, 1)
    head_cols = unit_columns(own_head)[0].astype(jnp.bfloat16)

    expo_s, raw, part, kept, teach_rows, high, low = student_pass(packet, stud, teach, head_cols, head_cols.T)
    targets, totals = sinkhorn(
        dp, protos, teach_rows, teach_cols, part.reshape(dp * stud // 128, 128)
    )
    totals = totals.reshape(dp, stud)
    aim = dot(head_cols, targets, 1, 1)
    scaled = (kept.astype(jnp.float32) / totals.reshape(1, dp * stud)).astype(jnp.bfloat16)
    head_grad, raw, aim = weight_pass(
        dp, protos, scale, expo_s, targets, own_head, scaled, high, low, raw, aim
    )

    share = width // protos
    offset = lax.axis_index("proto") * share
    view_lanes = (view == 1).reshape(1, crops, images)
    aims = aim.reshape(share, 2, 1, images)
    picked = jnp.where(view_lanes, aims[:, 1], aims[:, 0]).reshape(share, stud)
    own_part = (raw / lax.dynamic_index_in_dim(totals, me, 0, True) - picked) * scale
    own_unit = lax.dynamic_slice_in_dim(stud_unit, offset, share, 1).T
    along = lax.psum(jnp.sum(own_unit * own_part, axis=0, keepdims=True), "proto")
    student_grad = (own_part - own_unit * along).T * stud_inverse
    return (student_grad, head_grad)


def solution(mesh):
    return jax.shard_map(
        body,
        mesh=mesh,
        in_specs=(P("dp", None), P("dp", None), P(None, "proto"), P(None, "proto"), P("dp")),
        out_specs=(P("dp", "proto"), P("dp", "proto")),
        check_vma=False,
    )
```

```python
import functools
import math

import jax
import jax.numpy as jnp
from jax import lax
from jax.experimental import pallas as pl
from jax.experimental.layout import Layout, with_layout_constraint
from jax.experimental.pallas import tpu as pltpu
from jax.sharding import PartitionSpec as P

ITERS = 3


tiny_eps = 1e-06
teacher_temp = 0.04
student_temp = 0.1
BOTH = ("dp", "proto")


def unit_rows(values):
    floats = values.astype(jnp.float32)
    inverse = lax.rsqrt(jnp.sum(floats * floats, axis=1, keepdims=True) + tiny_eps)
    return (floats * inverse, inverse)


def unit_columns(values):
    floats = values.astype(jnp.float32)
    inverse = lax.rsqrt(jnp.sum(floats * floats, axis=0, keepdims=True) + tiny_eps)
    return (floats * inverse, inverse)


def dot(a, b, da, db):
    return lax.dot_general(a, b, (((da,), (db,)), ((), ())), preferred_element_type=jnp.float32)


def split_sum(values):
    high = values.astype(jnp.bfloat16)
    return high, (values - high.astype(jnp.float32)).astype(jnp.bfloat16)


LOG2E = math.log2(math.e)
MIB = 1 << 20


def diagonal():
    shape = (128, 128)
    return lax.broadcasted_iota(jnp.int32, shape, 0) == lax.broadcasted_iota(jnp.int32, shape, 1)


def to_lanes(column):
    return jnp.sum(jnp.where(diagonal(), column, 0.0), axis=0, keepdims=True)


def to_column(lanes):
    return jnp.sum(jnp.where(diagonal(), lanes, 0.0), axis=1, keepdims=True)


def chunks(size):
    step = min(size, 1024)
    return [(c, step) for c in range(0, size, step)]


def positions():
    return {"dp": lax.axis_index("dp"), "proto": lax.axis_index("proto")}


def greet(here, sizes):
    barrier = pltpu.get_barrier_semaphore()
    for axis, size in sizes.items():
        for k in range(1, size):
            pl.semaphore_signal(
                barrier,
                inc=1,
                device_id={axis: lax.rem(here[axis] + k, size)},
                device_id_type=pl.DeviceIdType.MESH,
            )
    pl.semaphore_wait(barrier, sum(sizes.values()) - len(sizes))


def sends(here, sizes, axis, source, target, sems):
    copies = []
    for k in range(1, sizes[axis]):
        peer = lax.rem(here[axis] + k, sizes[axis])
        copies.append(
            pltpu.make_async_remote_copy(
                src_ref=source(peer),
                dst_ref=target(k),
                send_sem=sems.at[0, k],
                recv_sem=sems.at[1, k],
                device_id={axis: peer},
                device_id_type=pl.DeviceIdType.MESH,
            )
        )
    return copies


def start_all(copies):
    for copy in copies:
        copy.start()
    return copies


def wait_all(copies):
    for copy in copies:
        copy.wait()


def exchange(here, sizes, axis, buffer, sems):
    wait_all(start_all(sends(here, sizes, axis, lambda peer: buffer.at[0], lambda k: buffer.at[k], sems)))
    total = buffer[0]
    for k in range(1, sizes[axis]):
        total = total + buffer[k]
    return total


def student_kernel(
    dp,
    protos,
    rows_ref,
    sums_ref,
    cols_ref,
    cols_t_ref,
    expo_ref,
    raw_ref,
    total_ref,
    kept_ref,
    high_ref,
    low_ref,
    near,
    far,
    near_sems,
    far_sems,
):
    turn = pl.program_id(0)
    rows = rows_ref[0].astype(jnp.bfloat16)
    kept_ref[...] = rows_ref[0].T.astype(jnp.bfloat16)
    high_ref[...], low_ref[...] = split_sum(sums_ref[0].T)
    raw, total = None, None
    for start, step in chunks(cols_ref.shape[1]):
        logits = dot(rows, cols_ref[:, start : start + step], 1, 0)
        expo = jnp.exp2(logits * (LOG2E / student_temp))
        part = jnp.sum(expo, axis=1, keepdims=True)
        kept = expo.astype(jnp.bfloat16)
        expo_ref[:, start : start + step] = kept
        grad = dot(kept, cols_t_ref[start : start + step, :], 1, 0)
        total = part if total is None else total + part
        raw = grad if raw is None else raw + grad
    raw_ref[...] = raw.T
    tiles = rows.shape[0] // 128
    for j in range(tiles):
        near[0, pl.ds(turn * tiles + j, 1), :] = to_lanes(total[j * 128 : (j + 1) * 128])

    @pl.when(turn == dp - 1)
    def _():
        here, sizes = positions(), {"dp": dp, "proto": protos}
        greet(here, sizes)
        far[0] = exchange(here, sizes, "proto", near, near_sems)
        total_ref[...] = exchange(here, sizes, "dp", far, far_sems)


def student_pass(protos, packet, stud, teach, cols, cols_t):
    dp, _, width = packet.shape
    first = stud // teach
    count = dp * stud
    assert stud == first * teach
    mine = cols.shape[1]
    return pl.pallas_call(
        functools.partial(student_kernel, dp, protos),
        grid=(dp,),
        in_specs=[
            pl.BlockSpec((1, stud, width), lambda i: (i, 0, 0)),
            pl.BlockSpec((1, teach, width), lambda i: (i, first, 0)),
            pl.BlockSpec((width, mine), lambda i: (0, 0)),
            pl.BlockSpec((mine, width), lambda i: (0, 0)),
        ],
        out_specs=[
            pl.BlockSpec((stud, mine), lambda i: (i, 0)),
            pl.BlockSpec((width, stud), lambda i: (0, i)),
            pl.BlockSpec((count // 128, 128), lambda i: (0, 0)),
            pl.BlockSpec((width, stud), lambda i: (0, i)),
            pl.BlockSpec((width, teach), lambda i: (0, i)),
            pl.BlockSpec((width, teach), lambda i: (0, i)),
        ],
        out_shape=[
            jax.ShapeDtypeStruct((dp * stud, mine), jnp.bfloat16),
            jax.ShapeDtypeStruct((width, dp * stud), jnp.float32),
            jax.ShapeDtypeStruct((count // 128, 128), jnp.float32),
            jax.ShapeDtypeStruct((width, dp * stud), jnp.bfloat16),
            jax.ShapeDtypeStruct((width, dp * teach), jnp.bfloat16),
            jax.ShapeDtypeStruct((width, dp * teach), jnp.bfloat16),
        ],
        scratch_shapes=[
            pltpu.VMEM((protos, count // 128, 128), jnp.float32),
            pltpu.VMEM((dp, count // 128, 128), jnp.float32),
            pltpu.SemaphoreType.DMA((2, protos)),
            pltpu.SemaphoreType.DMA((2, dp)),
        ],
        compiler_params=pltpu.CompilerParams(
            collective_id=3, has_side_effects=True, vmem_limit_bytes=52 * MIB
        ),
        cost_estimate=pl.CostEstimate(
            flops=4 * dp * stud * mine * width, bytes_accessed=2 * dp * stud * mine, transcendentals=dp * stud * mine
        ),
        name="student_pass",
    )(packet, packet, cols, cols_t)


def sinkhorn_kernel(
    dp,
    protos,
    rows_ref,
    cols_ref,
    targets_ref,
    total_ref,
    expo,
    cols,
    near,
    far,
    near_sems,
    far_sems,
):
    here, sizes = positions(), {"dp": dp, "proto": protos}
    greet(here, sizes)
    count, mine = expo.shape
    blocks = count // 128

    def rows_at(block):
        return pl.ds(pl.multiple_of(block * 128, 128), 128)

    cols[...] = jnp.zeros_like(cols)

    @pl.loop(0, blocks)
    def _(block):
        at = rows_at(block)
        for start, step in chunks(mine):
            values = jnp.exp2(
                dot(rows_ref[at, :].astype(jnp.bfloat16), cols_ref[:, start : start + step], 1, 0) * (LOG2E / teacher_temp)
            )
            expo[at, start : start + step] = values
            cols[:, start : start + step] += jnp.sum(values, axis=0, keepdims=True)

    for it in range(ITERS):
        if it:
            cols[...] = jnp.zeros_like(cols)

            @pl.loop(0, blocks)
            def _(block):
                at = rows_at(block)
                scale = to_column(total_ref[pl.ds(block, 1), :])
                cols[...] += jnp.sum(expo[at, :] * scale, axis=0, keepdims=True)

        cols[...] = 1.0 / cols[...]

        @pl.loop(0, blocks)
        def _(block):
            sums = jnp.sum(expo[rows_at(block), :] * cols[...], axis=1, keepdims=True)
            near[it, 0, pl.ds(block, 1), :] = to_lanes(sums)

        far[it, 0] = exchange(here, sizes, "proto", near.at[it], near_sems.at[it])
        total_ref[...] = 1.0 / exchange(here, sizes, "dp", far.at[it], far_sems.at[it])

    @pl.loop(0, blocks)
    def _(block):
        at = rows_at(block)
        scale = to_column(total_ref[pl.ds(block, 1), :])
        targets_ref[at, :] = (expo[at, :] * scale * cols[...]).astype(jnp.bfloat16)


def sinkhorn(dp, protos, rows, cols):
    count, mine = rows.shape[0], cols.shape[1]
    used = count // 128
    vmem = pl.BlockSpec(memory_space=pltpu.VMEM)
    return pl.pallas_call(
        functools.partial(sinkhorn_kernel, dp, protos),
        in_specs=[vmem] * 2,
        out_specs=[vmem] * 2,
        out_shape=[
            jax.ShapeDtypeStruct((count, mine), jnp.bfloat16),
            jax.ShapeDtypeStruct((used, 128), jnp.float32),
        ],
        scratch_shapes=[
            pltpu.VMEM((count, mine), jnp.float32),
            pltpu.VMEM((1, mine), jnp.float32),
            pltpu.VMEM((ITERS, protos, used, 128), jnp.float32),
            pltpu.VMEM((ITERS, dp, used, 128), jnp.float32),
            pltpu.SemaphoreType.DMA((ITERS, 2, protos)),
            pltpu.SemaphoreType.DMA((ITERS, 2, dp)),
        ],
        compiler_params=pltpu.CompilerParams(
            collective_id=1, has_side_effects=True, vmem_limit_bytes=52 * MIB
        ),
        cost_estimate=pl.CostEstimate(
            flops=2 * count * mine * rows.shape[1], bytes_accessed=40 * count * mine, transcendentals=count * mine
        ),
        name="sinkhorn",
    )(rows, cols)[0]


def weight_kernel(
    dp,
    protos,
    steps,
    scale,
    expo_ref,
    targets_ref,
    head_ref,
    rows_ref,
    high_ref,
    low_ref,
    raw_ref,
    aim_ref,
    grad_ref,
    raw_own_ref,
    aim_own_ref,
    stage,
    raw_near,
    raw_sum,
    raw_far,
    aim_near,
    aim_sum,
    aim_far,
    grad_sems,
    own_sem,
    raw_near_sems,
    raw_far_sems,
    near_sems,
    far_sems,
):
    here, sizes = positions(), {"dp": dp, "proto": protos}
    step = pl.program_id(0)
    share, stud = raw_own_ref.shape
    teach = aim_own_ref.shape[1]
    mine = stage.shape[1]
    size = head_ref.shape[1]
    depth = stage.shape[0] // dp

    def band(peer, height):
        return pl.ds(pl.multiple_of(peer * height, 8), height)

    def lanes(peer, length):
        return pl.ds(pl.multiple_of(peer * length, 128), length)

    raw_copies = sends(
        here, sizes, "dp", lambda e: raw_sum.at[:, lanes(e, stud)], lambda k: raw_far.at[k], raw_far_sems
    )
    each = dp // steps

    def block_copies(j):
        at = pl.ds(pl.multiple_of(j * each * stud, 128), each * stud)
        return sends(
            here,
            sizes,
            "proto",
            lambda e: raw_ref.at[band(e, share), at],
            lambda k: raw_near.at[k, :, at],
            raw_near_sems.at[j],
        )

    near_copies = sends(here, sizes, "proto", lambda e: aim_ref.at[band(e, share)], lambda k: aim_near.at[k], near_sems)
    far_copies = sends(here, sizes, "dp", lambda e: aim_sum.at[:, lanes(e, teach)], lambda k: aim_far.at[k], far_sems)

    def columns(j):
        return pl.ds(pl.multiple_of(here["dp"] * mine + j * size, 128), size)

    def grad_copies(j):
        local = pl.ds(pl.multiple_of(j * size, 128), size)
        return sends(
            here,
            sizes,
            "dp",
            lambda e: stage.at[band(e, depth), local],
            lambda k: grad_ref.at[:, columns(j)],
            grad_sems.at[j],
        )

    @pl.when(step == 0)
    def _():
        greet(here, sizes)
        start_all(near_copies)

    targets = targets_ref[...]
    grad = dot(rows_ref[...], expo_ref[...], 1, 0) - dot(high_ref[...], targets, 1, 0) - dot(low_ref[...], targets, 1, 0)
    grad = grad * scale
    unit, inverse = unit_columns(head_ref[...])
    inner = jnp.sum(unit * grad, axis=0, keepdims=True)
    stage[:, pl.ds(pl.multiple_of(step * size, 128), size)] = (grad - unit * inner) * inverse
    start_all(grad_copies(step))
    start_all(block_copies(step))

    @pl.when(step == steps - 1)
    def _():
        own = pltpu.make_async_copy(
            stage.at[band(here["dp"], depth)],
            grad_ref.at[:, pl.ds(pl.multiple_of(here["dp"] * mine, 128), mine)],
            own_sem,
        )
        own.start()
        wait_all(near_copies)
        total = aim_ref[band(here["proto"], share), :]
        for k in range(1, protos):
            total = total + aim_near[k]
        aim_sum[...] = total
        start_all(far_copies)
        for j in range(steps):
            wait_all(block_copies(j))
        total = raw_ref[band(here["proto"], share), :]
        for k in range(1, protos):
            total = total + raw_near[k]
        raw_sum[...] = total
        start_all(raw_copies)
        wait_all(raw_copies)
        total = raw_sum[:, lanes(here["dp"], stud)]
        for k in range(1, dp):
            total = total + raw_far[k]
        raw_own_ref[...] = total
        wait_all(far_copies)
        total = aim_sum[:, lanes(here["dp"], teach)]
        for k in range(1, dp):
            total = total + aim_far[k]
        aim_own_ref[...] = total
        own.wait()
        for j in range(steps):
            wait_all(grad_copies(j))


def weight_pass(dp, protos, scale, expo, targets, head, rows, high, low, raw, aim):
    width, mine = head.shape
    count, teach = rows.shape[1], high.shape[1]
    size = min(mine, 512)
    steps = mine // size
    assert dp % steps == 0
    share = width // protos

    def whole(array):
        return pl.BlockSpec(array.shape, lambda i: (0, 0))

    def block(array):
        return pl.BlockSpec((array.shape[0], size), lambda i: (0, i))

    own = [(share, count // dp), (share, teach // dp)]
    return pl.pallas_call(
        functools.partial(weight_kernel, dp, protos, steps, scale),
        grid=(steps,),
        in_specs=[block(expo), block(targets), block(head)]
        + [whole(x) for x in (rows, high, low)]
        + [pl.BlockSpec(memory_space=pltpu.VMEM)] * 2,
        out_specs=[pl.BlockSpec(memory_space=pl.ANY)] + [pl.BlockSpec(shape, lambda i: (0, 0)) for shape in own],
        out_shape=[jax.ShapeDtypeStruct(shape, jnp.float32) for shape in [(width // dp, dp * mine)] + own],
        scratch_shapes=[
            pltpu.VMEM((width, mine), jnp.float32),
            pltpu.VMEM((protos, share, count), jnp.float32),
            pltpu.VMEM((share, count), jnp.float32),
            pltpu.VMEM((dp,) + own[0], jnp.float32),
            pltpu.VMEM((protos, share, teach), jnp.float32),
            pltpu.VMEM((share, teach), jnp.float32),
            pltpu.VMEM((dp,) + own[1], jnp.float32),
            pltpu.SemaphoreType.DMA((steps, 2, dp)),
            pltpu.SemaphoreType.DMA,
            pltpu.SemaphoreType.DMA((steps, 2, protos)),
            pltpu.SemaphoreType.DMA((2, dp)),
            pltpu.SemaphoreType.DMA((2, protos)),
            pltpu.SemaphoreType.DMA((2, dp)),
        ],
        compiler_params=pltpu.CompilerParams(
            collective_id=2, has_side_effects=True, vmem_limit_bytes=52 * MIB
        ),
        cost_estimate=pl.CostEstimate(
            flops=2 * count * mine * width, bytes_accessed=2 * count * mine, transcendentals=0
        ),
        name="weight_pass",
    )(expo, targets, head, rows, high, low, raw, aim)


def body(teacher_feat, student_feat, teacher_weight, head_weight, pairing):
    dp, me = lax.axis_size("dp"), lax.axis_index("dp")
    protos = lax.axis_size("proto")
    teach, width = teacher_feat.shape
    stud = student_feat.shape[0]
    images = teach // 2
    crops = stud // images
    mine = head_weight.shape[1] // dp
    scale = 1.0 / (student_temp * stud * dp)

    teach_unit = unit_rows(teacher_feat)[0]
    stud_unit, stud_inverse = unit_rows(student_feat)
    view = (pairing - me * teach) // images
    kept = stud_unit.astype(jnp.bfloat16).astype(jnp.float32).reshape(crops, images, width)
    second = (view == 1).reshape(crops, images, 1)
    pair_sums = jnp.concatenate(
        [jnp.sum(jnp.where(second, 0.0, kept), 0), jnp.sum(jnp.where(second, kept, 0.0), 0)], 0
    )
    teach_rows = lax.all_gather(teach_unit, "dp", axis=0, tiled=True)
    packet = jnp.concatenate([stud_unit, pair_sums], 0)
    packet, teach_rows = lax.optimization_barrier((packet, teach_rows))
    packet = with_layout_constraint(packet, Layout(major_to_minor=(0, 1)))
    packet = lax.all_gather(packet, "dp", axis=0, tiled=False)
    teach_cols = unit_columns(lax.dynamic_slice_in_dim(teacher_weight, me * mine, mine, 1))[0].astype(jnp.bfloat16)
    own_head = lax.dynamic_slice_in_dim(head_weight, me * mine, mine, 1)
    head_cols = unit_columns(own_head)[0].astype(jnp.bfloat16)

    targets = sinkhorn(dp, protos, teach_rows, teach_cols)
    expo_s, raw, totals, kept, high, low = student_pass(protos, packet, stud, teach, head_cols, head_cols.T)
    totals = totals.reshape(dp, stud)
    aim = dot(head_cols, targets, 1, 1)
    scaled = (kept.astype(jnp.float32) / totals.reshape(1, dp * stud)).astype(jnp.bfloat16)
    head_grad, raw, aim = weight_pass(
        dp, protos, scale, expo_s, targets, own_head, scaled, high, low, raw, aim
    )

    share = width // protos
    offset = lax.axis_index("proto") * share
    view_lanes = (view == 1).reshape(1, crops, images)
    aims = aim.reshape(share, 2, 1, images)
    picked = jnp.where(view_lanes, aims[:, 1], aims[:, 0]).reshape(share, stud)
    own_part = (raw / lax.dynamic_index_in_dim(totals, me, 0, True) - picked) * scale
    own_unit = lax.dynamic_slice_in_dim(stud_unit, offset, share, 1).T
    along = lax.psum(jnp.sum(own_unit * own_part, axis=0, keepdims=True), "proto")
    student_grad = (own_part - own_unit * along).T * stud_inverse
    return (student_grad, head_grad)


def solution(mesh):
    return jax.shard_map(
        body,
        mesh=mesh,
        in_specs=(P("dp", None), P("dp", None), P(None, "proto"), P(None, "proto"), P("dp")),
        out_specs=(P("dp", "proto"), P("dp", "proto")),
        check_vma=False,
    )
```

```python
import functools
import math

import jax
import jax.numpy as jnp
from jax import lax
from jax.experimental import pallas as pl
from jax.experimental.layout import Layout, with_layout_constraint
from jax.experimental.pallas import tpu as pltpu
from jax.sharding import PartitionSpec as P

ITERS = 3


tiny_eps = 1e-06
teacher_temp = 0.04
student_temp = 0.1
BOTH = ("dp", "proto")


def unit_rows(values):
    floats = values.astype(jnp.float32)
    inverse = lax.rsqrt(jnp.sum(floats * floats, axis=1, keepdims=True) + tiny_eps)
    return (floats * inverse, inverse)


def unit_columns(values):
    floats = values.astype(jnp.float32)
    inverse = lax.rsqrt(jnp.sum(floats * floats, axis=0, keepdims=True) + tiny_eps)
    return (floats * inverse, inverse)


def dot(a, b, da, db):
    return lax.dot_general(a, b, (((da,), (db,)), ((), ())), preferred_element_type=jnp.float32)


def split_sum(values):
    high = values.astype(jnp.bfloat16)
    return high, (values - high.astype(jnp.float32)).astype(jnp.bfloat16)


LOG2E = math.log2(math.e)
MIB = 1 << 20


def diagonal():
    shape = (128, 128)
    return lax.broadcasted_iota(jnp.int32, shape, 0) == lax.broadcasted_iota(jnp.int32, shape, 1)


def to_lanes(column):
    return jnp.sum(jnp.where(diagonal(), column, 0.0), axis=0, keepdims=True)


def to_column(lanes):
    return jnp.sum(jnp.where(diagonal(), lanes, 0.0), axis=1, keepdims=True)


def chunks(size):
    step = min(size, 1024)
    return [(c, step) for c in range(0, size, step)]


def positions():
    return {"dp": lax.axis_index("dp"), "proto": lax.axis_index("proto")}


def greet(here, sizes):
    barrier = pltpu.get_barrier_semaphore()
    for axis, size in sizes.items():
        for k in range(1, size):
            pl.semaphore_signal(
                barrier,
                inc=1,
                device_id={axis: lax.rem(here[axis] + k, size)},
                device_id_type=pl.DeviceIdType.MESH,
            )
    pl.semaphore_wait(barrier, sum(sizes.values()) - len(sizes))


def sends(here, sizes, axis, source, target, sems):
    copies = []
    for k in range(1, sizes[axis]):
        peer = lax.rem(here[axis] + k, sizes[axis])
        copies.append(
            pltpu.make_async_remote_copy(
                src_ref=source(peer),
                dst_ref=target(k),
                send_sem=sems.at[0, k],
                recv_sem=sems.at[1, k],
                device_id={axis: peer},
                device_id_type=pl.DeviceIdType.MESH,
            )
        )
    return copies


def start_all(copies):
    for copy in copies:
        copy.start()
    return copies


def wait_all(copies):
    for copy in copies:
        copy.wait()


def exchange(here, sizes, axis, buffer, sems):
    wait_all(start_all(sends(here, sizes, axis, lambda peer: buffer.at[0], lambda k: buffer.at[k], sems)))
    total = buffer[0]
    for k in range(1, sizes[axis]):
        total = total + buffer[k]
    return total


def student_kernel(
    dp,
    protos,
    rows_ref,
    sums_ref,
    cols_ref,
    cols_t_ref,
    expo_ref,
    raw_ref,
    total_ref,
    kept_ref,
    high_ref,
    low_ref,
    near,
    far,
    near_sems,
    far_sems,
):
    turn = pl.program_id(0)
    rows = rows_ref[0].astype(jnp.bfloat16)
    kept_ref[...] = rows_ref[0].T.astype(jnp.bfloat16)
    high_ref[...], low_ref[...] = split_sum(sums_ref[0].T)
    raw, total = None, None
    for start, step in chunks(cols_ref.shape[1]):
        logits = dot(rows, cols_ref[:, start : start + step], 1, 0)
        expo = jnp.exp2(logits * (LOG2E / student_temp))
        part = jnp.sum(expo, axis=1, keepdims=True)
        kept = expo.astype(jnp.bfloat16)
        expo_ref[:, start : start + step] = kept
        grad = dot(kept, cols_t_ref[start : start + step, :], 1, 0)
        total = part if total is None else total + part
        raw = grad if raw is None else raw + grad
    raw_ref[...] = raw.T
    tiles = rows.shape[0] // 128
    for j in range(tiles):
        near[0, pl.ds(turn * tiles + j, 1), :] = to_lanes(total[j * 128 : (j + 1) * 128])

    @pl.when(turn == dp - 1)
    def _():
        here, sizes = positions(), {"dp": dp, "proto": protos}
        greet(here, sizes)
        far[0] = exchange(here, sizes, "proto", near, near_sems)
        total_ref[...] = exchange(here, sizes, "dp", far, far_sems)


def student_pass(protos, packet, stud, teach, cols, cols_t):
    dp, _, width = packet.shape
    first = stud // teach
    count = dp * stud
    assert stud == first * teach
    mine = cols.shape[1]
    return pl.pallas_call(
        functools.partial(student_kernel, dp, protos),
        grid=(dp,),
        in_specs=[
            pl.BlockSpec((1, stud, width), lambda i: (i, 0, 0)),
            pl.BlockSpec((1, teach, width), lambda i: (i, first, 0)),
            pl.BlockSpec((width, mine), lambda i: (0, 0)),
            pl.BlockSpec((mine, width), lambda i: (0, 0)),
        ],
        out_specs=[
            pl.BlockSpec((stud, mine), lambda i: (i, 0)),
            pl.BlockSpec((width, stud), lambda i: (0, i)),
            pl.BlockSpec((count // 128, 128), lambda i: (0, 0)),
            pl.BlockSpec((width, stud), lambda i: (0, i)),
            pl.BlockSpec((width, teach), lambda i: (0, i)),
            pl.BlockSpec((width, teach), lambda i: (0, i)),
        ],
        out_shape=[
            jax.ShapeDtypeStruct((dp * stud, mine), jnp.bfloat16),
            jax.ShapeDtypeStruct((width, dp * stud), jnp.float32),
            jax.ShapeDtypeStruct((count // 128, 128), jnp.float32),
            jax.ShapeDtypeStruct((width, dp * stud), jnp.bfloat16),
            jax.ShapeDtypeStruct((width, dp * teach), jnp.bfloat16),
            jax.ShapeDtypeStruct((width, dp * teach), jnp.bfloat16),
        ],
        scratch_shapes=[
            pltpu.VMEM((protos, count // 128, 128), jnp.float32),
            pltpu.VMEM((dp, count // 128, 128), jnp.float32),
            pltpu.SemaphoreType.DMA((2, protos)),
            pltpu.SemaphoreType.DMA((2, dp)),
        ],
        compiler_params=pltpu.CompilerParams(
            collective_id=3, has_side_effects=True, vmem_limit_bytes=52 * MIB
        ),
        cost_estimate=pl.CostEstimate(
            flops=4 * dp * stud * mine * width, bytes_accessed=2 * dp * stud * mine, transcendentals=dp * stud * mine
        ),
        name="student_pass",
    )(packet, packet, cols, cols_t)


def sinkhorn_kernel(
    dp,
    protos,
    rows_ref,
    cols_ref,
    targets_ref,
    total_ref,
    expo,
    cols,
    near,
    far,
    near_sems,
    far_sems,
):
    here, sizes = positions(), {"dp": dp, "proto": protos}
    greet(here, sizes)
    count, mine = expo.shape
    blocks = count // 128

    def rows_at(block):
        return pl.ds(pl.multiple_of(block * 128, 128), 128)

    cols[...] = jnp.zeros_like(cols)

    @pl.loop(0, blocks)
    def _(block):
        at = rows_at(block)
        for start, step in chunks(mine):
            values = jnp.exp2(
                dot(rows_ref[at, :].astype(jnp.bfloat16), cols_ref[:, start : start + step], 1, 0) * (LOG2E / teacher_temp)
            )
            expo[at, start : start + step] = values
            cols[:, start : start + step] += jnp.sum(values, axis=0, keepdims=True)

    for it in range(ITERS):
        if it:
            cols[...] = jnp.zeros_like(cols)

            @pl.loop(0, blocks)
            def _(block):
                at = rows_at(block)
                scale = to_column(total_ref[pl.ds(block, 1), :])
                cols[...] += jnp.sum(expo[at, :] * scale, axis=0, keepdims=True)

        cols[...] = 1.0 / cols[...]

        @pl.loop(0, blocks)
        def _(block):
            sums = jnp.sum(expo[rows_at(block), :] * cols[...], axis=1, keepdims=True)
            near[it, 0, pl.ds(block, 1), :] = to_lanes(sums)

        far[it, 0] = exchange(here, sizes, "proto", near.at[it], near_sems.at[it])
        total_ref[...] = 1.0 / exchange(here, sizes, "dp", far.at[it], far_sems.at[it])

    @pl.loop(0, blocks)
    def _(block):
        at = rows_at(block)
        scale = to_column(total_ref[pl.ds(block, 1), :])
        targets_ref[at, :] = (expo[at, :] * scale * cols[...]).astype(jnp.bfloat16)


def sinkhorn(dp, protos, rows, cols):
    count, mine = rows.shape[0], cols.shape[1]
    used = count // 128
    vmem = pl.BlockSpec(memory_space=pltpu.VMEM)
    return pl.pallas_call(
        functools.partial(sinkhorn_kernel, dp, protos),
        in_specs=[vmem] * 2,
        out_specs=[vmem] * 2,
        out_shape=[
            jax.ShapeDtypeStruct((count, mine), jnp.bfloat16),
            jax.ShapeDtypeStruct((used, 128), jnp.float32),
        ],
        scratch_shapes=[
            pltpu.VMEM((count, mine), jnp.float32),
            pltpu.VMEM((1, mine), jnp.float32),
            pltpu.VMEM((ITERS, protos, used, 128), jnp.float32),
            pltpu.VMEM((ITERS, dp, used, 128), jnp.float32),
            pltpu.SemaphoreType.DMA((ITERS, 2, protos)),
            pltpu.SemaphoreType.DMA((ITERS, 2, dp)),
        ],
        compiler_params=pltpu.CompilerParams(
            collective_id=1, has_side_effects=True, vmem_limit_bytes=52 * MIB
        ),
        cost_estimate=pl.CostEstimate(
            flops=2 * count * mine * rows.shape[1], bytes_accessed=40 * count * mine, transcendentals=count * mine
        ),
        name="sinkhorn",
    )(rows, cols)[0]


def weight_kernel(
    dp,
    protos,
    steps,
    scale,
    expo_ref,
    targets_ref,
    head_ref,
    rows_ref,
    high_ref,
    low_ref,
    raw_ref,
    aim_ref,
    grad_ref,
    raw_own_ref,
    aim_own_ref,
    stage,
    raw_near,
    raw_sum,
    raw_far,
    aim_near,
    aim_sum,
    aim_far,
    grad_sems,
    own_sem,
    raw_near_sems,
    raw_far_sems,
    near_sems,
    far_sems,
):
    here, sizes = positions(), {"dp": dp, "proto": protos}
    step = pl.program_id(0)
    share, stud = raw_own_ref.shape
    teach = aim_own_ref.shape[1]
    mine = stage.shape[1]
    size = head_ref.shape[1]
    depth = stage.shape[0] // dp

    def band(peer, height):
        return pl.ds(pl.multiple_of(peer * height, 8), height)

    def lanes(peer, length):
        return pl.ds(pl.multiple_of(peer * length, 128), length)

    raw_copies = sends(
        here, sizes, "dp", lambda e: raw_sum.at[:, lanes(e, stud)], lambda k: raw_far.at[k], raw_far_sems
    )
    each = dp // steps

    def block_copies(j):
        at = pl.ds(pl.multiple_of(j * each * stud, 128), each * stud)
        return sends(
            here,
            sizes,
            "proto",
            lambda e: raw_ref.at[band(e, share), at],
            lambda k: raw_near.at[k, :, at],
            raw_near_sems.at[j],
        )

    near_copies = sends(here, sizes, "proto", lambda e: aim_ref.at[band(e, share)], lambda k: aim_near.at[k], near_sems)
    far_copies = sends(here, sizes, "dp", lambda e: aim_sum.at[:, lanes(e, teach)], lambda k: aim_far.at[k], far_sems)

    def columns(j):
        return pl.ds(pl.multiple_of(here["dp"] * mine + j * size, 128), size)

    def grad_copies(j):
        local = pl.ds(pl.multiple_of(j * size, 128), size)
        return sends(
            here,
            sizes,
            "dp",
            lambda e: stage.at[band(e, depth), local],
            lambda k: grad_ref.at[:, columns(j)],
            grad_sems.at[j],
        )

    @pl.when(step == 0)
    def _():
        greet(here, sizes)
        start_all(near_copies)

    targets = targets_ref[...]
    grad = dot(rows_ref[...], expo_ref[...], 1, 0) - dot(high_ref[...], targets, 1, 0) - dot(low_ref[...], targets, 1, 0)
    grad = grad * scale
    unit, inverse = unit_columns(head_ref[...])
    inner = jnp.sum(unit * grad, axis=0, keepdims=True)
    stage[:, pl.ds(pl.multiple_of(step * size, 128), size)] = (grad - unit * inner) * inverse
    start_all(grad_copies(step))
    start_all(block_copies(step))

    @pl.when(step == steps - 1)
    def _():
        own = pltpu.make_async_copy(
            stage.at[band(here["dp"], depth)],
            grad_ref.at[:, pl.ds(pl.multiple_of(here["dp"] * mine, 128), mine)],
            own_sem,
        )
        own.start()
        wait_all(near_copies)
        total = aim_ref[band(here["proto"], share), :]
        for k in range(1, protos):
            total = total + aim_near[k]
        aim_sum[...] = total
        start_all(far_copies)
        for j in range(steps):
            wait_all(block_copies(j))
        total = raw_ref[band(here["proto"], share), :]
        for k in range(1, protos):
            total = total + raw_near[k]
        raw_sum[...] = total
        start_all(raw_copies)
        wait_all(raw_copies)
        total = raw_sum[:, lanes(here["dp"], stud)]
        for k in range(1, dp):
            total = total + raw_far[k]
        raw_own_ref[...] = total
        wait_all(far_copies)
        total = aim_sum[:, lanes(here["dp"], teach)]
        for k in range(1, dp):
            total = total + aim_far[k]
        aim_own_ref[...] = total
        own.wait()
        for j in range(steps):
            wait_all(grad_copies(j))


def weight_pass(dp, protos, scale, expo, targets, head, rows, high, low, raw, aim):
    width, mine = head.shape
    count, teach = rows.shape[1], high.shape[1]
    size = min(mine, 512)
    steps = mine // size
    assert dp % steps == 0
    share = width // protos

    def whole(array):
        return pl.BlockSpec(array.shape, lambda i: (0, 0))

    def block(array):
        return pl.BlockSpec((array.shape[0], size), lambda i: (0, i))

    own = [(share, count // dp), (share, teach // dp)]
    return pl.pallas_call(
        functools.partial(weight_kernel, dp, protos, steps, scale),
        grid=(steps,),
        in_specs=[block(expo), block(targets), block(head)]
        + [whole(x) for x in (rows, high, low)]
        + [pl.BlockSpec(memory_space=pltpu.VMEM)] * 2,
        out_specs=[pl.BlockSpec(memory_space=pl.ANY)] + [pl.BlockSpec(shape, lambda i: (0, 0)) for shape in own],
        out_shape=[jax.ShapeDtypeStruct(shape, jnp.float32) for shape in [(width // dp, dp * mine)] + own],
        scratch_shapes=[
            pltpu.VMEM((width, mine), jnp.float32),
            pltpu.VMEM((protos, share, count), jnp.float32),
            pltpu.VMEM((share, count), jnp.float32),
            pltpu.VMEM((dp,) + own[0], jnp.float32),
            pltpu.VMEM((protos, share, teach), jnp.float32),
            pltpu.VMEM((share, teach), jnp.float32),
            pltpu.VMEM((dp,) + own[1], jnp.float32),
            pltpu.SemaphoreType.DMA((steps, 2, dp)),
            pltpu.SemaphoreType.DMA,
            pltpu.SemaphoreType.DMA((steps, 2, protos)),
            pltpu.SemaphoreType.DMA((2, dp)),
            pltpu.SemaphoreType.DMA((2, protos)),
            pltpu.SemaphoreType.DMA((2, dp)),
        ],
        compiler_params=pltpu.CompilerParams(
            collective_id=2, has_side_effects=True, vmem_limit_bytes=52 * MIB
        ),
        cost_estimate=pl.CostEstimate(
            flops=2 * count * mine * width, bytes_accessed=2 * count * mine, transcendentals=0
        ),
        name="weight_pass",
    )(expo, targets, head, rows, high, low, raw, aim)


def body(teacher_feat, student_feat, teacher_weight, head_weight, pairing):
    dp, me = lax.axis_size("dp"), lax.axis_index("dp")
    protos = lax.axis_size("proto")
    teach, width = teacher_feat.shape
    stud = student_feat.shape[0]
    images = teach // 2
    crops = stud // images
    mine = head_weight.shape[1] // dp
    scale = 1.0 / (student_temp * stud * dp)

    teach_unit = unit_rows(teacher_feat)[0]
    stud_unit, stud_inverse = unit_rows(student_feat)
    view = (pairing - me * teach) // images
    kept = stud_unit.astype(jnp.bfloat16).astype(jnp.float32).reshape(crops, images, width)
    second = (view == 1).reshape(crops, images, 1)
    pair_sums = jnp.concatenate(
        [jnp.sum(jnp.where(second, 0.0, kept), 0), jnp.sum(jnp.where(second, kept, 0.0), 0)], 0
    )
    teach_rows = lax.all_gather(teach_unit, "dp", axis=0, tiled=True)
    packet = jnp.concatenate([stud_unit, pair_sums], 0)
    teach_cols = unit_columns(lax.dynamic_slice_in_dim(teacher_weight, me * mine, mine, 1))[0].astype(jnp.bfloat16)
    own_head = lax.dynamic_slice_in_dim(head_weight, me * mine, mine, 1)
    head_cols = unit_columns(own_head)[0].astype(jnp.bfloat16)
    head_cols_t = head_cols.T
    packet, teach_rows, teach_cols, head_cols, head_cols_t, own_head = lax.optimization_barrier(
        (packet, teach_rows, teach_cols, head_cols, head_cols_t, own_head)
    )
    packet = with_layout_constraint(packet, Layout(major_to_minor=(0, 1)))
    packet = lax.all_gather(packet, "dp", axis=0, tiled=False)

    targets = sinkhorn(dp, protos, teach_rows, teach_cols)
    expo_s, raw, totals, kept, high, low = student_pass(protos, packet, stud, teach, head_cols, head_cols_t)
    totals = totals.reshape(dp, stud)
    aim = dot(head_cols, targets, 1, 1)
    scaled = (kept.astype(jnp.float32) / totals.reshape(1, dp * stud)).astype(jnp.bfloat16)
    head_grad, raw, aim = weight_pass(
        dp, protos, scale, expo_s, targets, own_head, scaled, high, low, raw, aim
    )

    share = width // protos
    offset = lax.axis_index("proto") * share
    view_lanes = (view == 1).reshape(1, crops, images)
    aims = aim.reshape(share, 2, 1, images)
    picked = jnp.where(view_lanes, aims[:, 1], aims[:, 0]).reshape(share, stud)
    own_part = (raw / lax.dynamic_index_in_dim(totals, me, 0, True) - picked) * scale
    own_unit = lax.dynamic_slice_in_dim(stud_unit, offset, share, 1).T
    along = lax.psum(jnp.sum(own_unit * own_part, axis=0, keepdims=True), "proto")
    student_grad = (own_part - own_unit * along).T * stud_inverse
    return (student_grad, head_grad)


def solution(mesh):
    return jax.shard_map(
        body,
        mesh=mesh,
        in_specs=(P("dp", None), P("dp", None), P(None, "proto"), P(None, "proto"), P("dp")),
        out_specs=(P("dp", "proto"), P("dp", "proto")),
        check_vma=False,
    )
```
